512 devices in a mesh: batch: 16 (over z_lo, x), seq: 32 (over y, z_hi, core).
Axes of the slice: x: 4, y: 4, z: 16 (z_hi: 4, z_lo: 4; z = z_hi * 4 + z_lo), core: 2. Of those that a mesh axis runs over, the one named last changes fastest.
Arguments:
- tokens: bfloat16 [16, 4096, 1536], P('batch', 'seq'), may hold values from -6 to 6
- norm_gain: float32 [1536], replicated, may hold values from 0.1 to 1.9
- w_query: bfloat16 [1536, 512], P('batch'), may hold values from -4 to 4
- w_keyval: bfloat16 [1536, 256], P('batch'), may hold values from -1 to 1
- w_out: bfloat16 [512, 1536], P('batch'), may hold values from -0.25 to 0.25
- cotangent: bfloat16 [16, 4096, 1536], P('batch', 'seq'), may hold values from -6 to 6
Outputs:
- layer_out: bfloat16 [16, 4096, 1536], P('batch', 'seq')
- input_grad: bfloat16 [16, 4096, 1536], P('batch', 'seq')
- keyval_grad: float32 [1536, 256], P('batch')
The draws below stay inside these ranges and needn't reach their ends.
All inputs are finite; a program needn't handle non-finite values.
Results may differ from the reference program's by a relative error of at most 0.013.
Values may be sent and summed in bfloat16 or wider, within the bound.
A program may use at most 64 MiB of HBM per device.

```python
import math
import jax
import jax.numpy as jnp
from jax import lax

D = 1536
HEADS = 4
HD = 128
TOK_DEV = 128
SEQ = 4096
BATCH = 16
N_SEQ = 32


def key_columns(key):
    return jax.random.normal(key, (D, HD), jnp.float32) * D ** (-0.5)


def draw_w_keyval(key, part):
    shared = key_columns(key)
    key = jax.random.fold_in(key, 11)
    value_cols = jax.random.normal(key, (D, HD), jnp.float32) * D ** (-0.5)
    return jnp.clip(jnp.concatenate([shared, value_cols], axis=1), -1.0, 1.0).astype(jnp.bfloat16)


def draw_w_query(key, part):
    key = jax.random.fold_in(key, 7)
    first_key = jax.random.fold_in(key, 0)
    noise = jax.random.normal(first_key, (D, HEADS * HD), jnp.float32) * D ** (-0.5)
    result = noise
    return jnp.clip(result, -4.0, 4.0).astype(jnp.bfloat16)


def steps_of(key, dims, cuts, smallest, largest):
    def one(dim, parts):
        heights = jax.random.uniform(jax.random.fold_in(jax.random.fold_in(key, 6), dim), (parts,), jnp.float32, smallest / len(cuts), largest / len(cuts))
        return jnp.repeat(jnp.exp(heights), dims[dim] // parts).reshape((-1,) + (1,) * (len(dims) - dim - 1))

    gain = one(*cuts[0])
    for cut in cuts[1:]:
        gain = gain * one(*cut)
    return gain


def scatter_about(key, shape, width, most, cuts=(), dtype=jnp.bfloat16):
    factor_of = steps_of(key, shape, cuts, -0.22, 0.18) if cuts else 1.0
    values = jax.random.normal(key, shape, jnp.float32) * width * factor_of
    return jnp.minimum(jnp.maximum(values, -most), most).astype(dtype)


def setup_inputs(seed: int = 0) -> dict:
    splits = jax.random.split(jax.random.key(seed), 7)
    tokens = scatter_about(splits[0], (BATCH, SEQ, D), 1.0, 6.0, ((0, 16), (1, 32)))
    norm_gain = jnp.clip(1.0 + 0.18 * jax.random.normal(splits[1], (D,), jnp.float32), 0.1, 1.9)
    w_query = draw_w_query(jax.random.fold_in(splits[6], 71), 0)
    w_keyval = draw_w_keyval(jax.random.fold_in(splits[6], 71), 0)
    w_out = scatter_about(splits[4], (HEADS * HD, D), (HEADS * HD) ** -0.5, 0.25, ((0, 16),))
    cotangent = scatter_about(splits[5], (BATCH, SEQ, D), 1.0, 6.0, ((0, 16), (1, 32)))
    return dict(tokens=tokens, norm_gain=norm_gain, w_query=w_query, w_keyval=w_keyval, w_out=w_out, cotangent=cotangent)


epsilon = 1e-06

def per_example(tokens_row, cotangent_row, norm_gain, w_query, w_keyval, w_out):
    seq_total = tokens_row.shape[0]
    score_scale = 1.0 / math.sqrt(HD)
    tokens_f32 = tokens_row.astype(jnp.float32)
    inv_rms = lax.rsqrt(lax.optimization_barrier(jnp.mean(tokens_f32 * tokens_f32, axis=-1, keepdims=True)) + epsilon)
    unit_rows = tokens_f32 * inv_rms
    normed = (unit_rows * norm_gain).astype(jnp.bfloat16)
    queries = jnp.dot(normed, w_query, preferred_element_type=jnp.float32).astype(jnp.bfloat16)
    keyvalues = jnp.dot(normed, w_keyval, preferred_element_type=jnp.float32).astype(jnp.bfloat16)
    keys_f32 = keyvalues[:, :HD].astype(jnp.float32)
    values_f32 = keyvalues[:, HD:].astype(jnp.float32)
    query_heads = queries.reshape(seq_total, HEADS, HD).astype(jnp.float32)
    scores = jnp.einsum('ihd,jd->hij', query_heads, keys_f32) * score_scale
    prob_f32 = jax.nn.softmax(scores, axis=-1)
    probs_low = prob_f32.astype(jnp.bfloat16)
    attention_f = jnp.einsum('hij,jd->ihd', probs_low.astype(jnp.float32), values_f32)
    attention = attention_f.reshape(seq_total, HEADS * HD).astype(jnp.bfloat16)
    layer_rows = (tokens_f32 + jnp.dot(attention, w_out, preferred_element_type=jnp.float32)).astype(jnp.bfloat16)
    d_attention = jnp.dot(cotangent_row, w_out.T, preferred_element_type=jnp.float32).astype(jnp.bfloat16)
    d_heads = d_attention.reshape(seq_total, HEADS, HD).astype(jnp.float32)
    row_delta = lax.optimization_barrier(jnp.sum(d_heads * attention_f, axis=-1))
    d_probs = jnp.einsum('ihd,jd->hij', d_heads, values_f32)
    d_scores = (prob_f32 * (d_probs - row_delta.T[:, :, None])).astype(jnp.bfloat16)
    d_queries = jnp.einsum('hij,jd->ihd', d_scores.astype(jnp.float32), keys_f32) * score_scale
    d_queries = d_queries.reshape(seq_total, HEADS * HD).astype(jnp.bfloat16)
    score_shards = d_scores.astype(jnp.float32).reshape(HEADS, N_SEQ, TOK_DEV, seq_total)
    query_shards = query_heads.reshape(N_SEQ, TOK_DEV, HEADS, HD)
    key_partial = jnp.einsum('hnij,nihd->njd', score_shards, query_shards) * score_scale
    prob_shards = probs_low.astype(jnp.float32).reshape(HEADS, N_SEQ, TOK_DEV, seq_total)
    grad_shards = d_heads.reshape(N_SEQ, TOK_DEV, HEADS, HD)
    value_partial = jnp.einsum('hnij,nihd->njd', prob_shards, grad_shards)
    partials = jnp.concatenate([key_partial, value_partial], axis=-1).astype(jnp.bfloat16)
    partials = lax.optimization_barrier(partials).astype(jnp.float32)
    d_keyvalues = lax.optimization_barrier(jnp.sum(partials, axis=0)).astype(jnp.bfloat16)
    d_normed = jnp.dot(d_queries, w_query.T, preferred_element_type=jnp.float32)
    d_normed = d_normed + jnp.dot(d_keyvalues, w_keyval.T, preferred_element_type=jnp.float32)
    d_unit = d_normed * norm_gain
    input_rows = inv_rms * (d_unit - unit_rows * lax.optimization_barrier(jnp.mean(d_unit * unit_rows, axis=-1, keepdims=True)))
    grad_term = jnp.dot(normed.T, d_keyvalues, preferred_element_type=jnp.float32)
    return (layer_rows, input_rows.astype(jnp.bfloat16), grad_term)

def reference(tokens, norm_gain, w_query, w_keyval, w_out, cotangent):

    def one_example(pair):
        return per_example(pair[0], pair[1], norm_gain, w_query, w_keyval, w_out)
    layer_out, input_grad, grad_terms = lax.map(one_example, (tokens, cotangent))
    keyval_grad = lax.optimization_barrier(jnp.sum(grad_terms, axis=0)) / math.sqrt(BATCH * SEQ)
    return (layer_out, input_grad, keyval_grad)
```

```python
import math

import jax
import jax.numpy as jnp
from jax import lax
from jax.experimental import pallas as pl
from jax.experimental.pallas import tpu as pltpu
from jax.sharding import PartitionSpec as P

MESH = pl.DeviceIdType.MESH
BF, F32 = jnp.bfloat16, jnp.float32
EPS = 1e-06
HD, HEADS, TOK, D = 128, 4, 128, 1536
ROWS = HEADS * TOK
SCALE = 1.0 / math.sqrt(HD)
LOG2 = SCALE * math.log2(math.e)
NT_DIMS = (((1,), (1,)), ((), ()))
Y_ORDER = (0, 1, 3, 2)
Z_ORDER = (2, 1, 3, 0)


def mm(a, b):
    return jnp.dot(a, b, preferred_element_type=F32)


def mm_nt(a, b):
    return lax.dot_general(a, b, NT_DIMS, preferred_element_type=F32)


def rem4(v):
    return lax.rem(v, 4)


def kernel(
    tok_ref, gain_ref, wq_ref, wkv_ref, wo_ref, cot_ref,
    out_ref, ing_ref, kvg_ref,
    wkv, wq, wo, nrm, nt, kv, qs, qt, sbuf, ebuf, acc, mrow, mk, lrow,
    dos, dog, dot_, delta, att, dq, part, sib, mine, yrec, zsum, zrec,
    dtok, dkv, dn, gr, ra, gb, rb, yg, zg, fin,
    w1s, w2s, wss, wr, wsr, kzs, kys, kss, kvr, nts, ntr,
    rss, rsr, rys, ryr, rzs, rzr, ds_, dr_, gas, gar, gbs, gbr, ygs, ygr, zgs, zgr, fs, fr,
):
    bi = lax.axis_index("batch")
    si = lax.axis_index("seq")
    zl, x = lax.div(bi, 4), rem4(bi)
    y, zh, c = lax.div(si, 8), rem4(lax.div(si, 2)), lax.rem(si, 2)

    def at(dx=0, dy=0, dz=0, dc=0):
        z = lax.rem(zh * 4 + zl + dz + 16, 16)
        return (
            rem4(z) * 4 + rem4(x + dx + 4),
            rem4(y + dy + 4) * 8 + lax.div(z, 4) * 2 + lax.rem(c + dc, 2),
        )

    sibling = at(dc=1)

    def rcopy(src, dst, ssem, rsem, device):
        return pltpu.make_async_remote_copy(
            src_ref=src, dst_ref=dst, send_sem=ssem, recv_sem=rsem, device_id=device, device_id_type=MESH
        )

    def wait_recv(ref, rsem):
        rcopy(ref, ref, rsem, rsem, sibling).wait_recv()

    def wait_send(ref, ssem):
        rcopy(ref, ref, ssem, ssem, sibling).wait_send()

    def loop(lo, hi, body):
        def step(i, carry):
            body(i)
            return carry

        lax.fori_loop(lo, hi, step, 0)

    barrier = pltpu.get_barrier_semaphore()
    partners = [at(dc=1)]
    partners += [at(dx=k) for k in (1, 2, 3)]
    partners += [at(dy=k) for k in (1, 2, 3)]
    partners += [at(dz=k) for k in (1, -1, 2, -2, 4, -4, 8)]
    for p in partners:
        pl.semaphore_signal(barrier, inc=1, device_id=p, device_id_type=MESH)

    for w_ref, w, h in ((wkv_ref, wkv, 48), (wq_ref, wq, 48), (wo_ref, wo, 16)):
        w[zl, x, 0] = w_ref[:h]
        w[zl, x, 1] = w_ref[h:]
    tok = tok_ref[...].astype(F32)
    inv = lax.rsqrt(jnp.mean(tok * tok, axis=-1, keepdims=True) + EPS)
    normed = tok * inv * gain_ref[...]
    nrm[...] = normed.astype(BF)
    for i in range(D // 128):
        nt[c, i * 128 : (i + 1) * 128, :] = normed[:, i * 128 : (i + 1) * 128].T.astype(BF)
    pl.semaphore_wait(barrier, len(partners))

    one = c * 0 + 1
    zero = c * 0
    weights = ((wkv, c, 1 - c), (wq, zero, one), (wo, zero, one))

    def block(w, i, j):
        ref, ax, az = weights[w]
        zz, xx = rem4(zl + i * az + j * ax), rem4(x + i * ax + j * az)
        return ref.at[zz, xx, c], zz * 4 + xx

    def other_half(w, i, j):
        ref, ax, az = weights[w]
        zz, xx = rem4(zl + i * az + j * ax), rem4(x + i * ax + j * az)
        return ref.at[zz, xx, 1 - c], zz * 4 + xx

    def zshift(k):
        return rem4(k + 1) - 1

    def first_send(w):
        ref, ax, az = weights[w]

        def body(k):
            src, idx = block(w, 0, 0)
            rcopy(src, src, w1s.at[w, k], wr.at[w, idx], at(dx=k * ax, dz=zshift(k) * az)).start()

        loop(1, 4, body)

    def to_sibling(w, i, j):
        src, idx = block(w, i, j)
        rcopy(src, src, wss.at[w, idx], wsr.at[w, idx], sibling).start()

    def first_arrive(w):
        def body(i):
            src, idx = block(w, i, 0)
            wait_recv(src, wr.at[w, idx])

        loop(1, 4, body)

    def second_send(w):
        ref, ax, az = weights[w]

        def body(i):
            src, idx = block(w, i, 0)
            for k in (1, 3, 2):
                rcopy(src, src, w2s.at[w, i * 4 + k], wr.at[w, idx], at(dx=k * az, dz=zshift(k) * ax)).start()

        loop(0, 4, body)
        loop(1, 4, lambda i: to_sibling(w, i, 0))

    def second_arrive(w):
        for j in (1, 3, 2):

            def body(i, j=j):
                src, idx = block(w, i, j)
                wait_recv(src, wr.at[w, idx])
                to_sibling(w, i, j)

            loop(0, 4, body)

    def sibling_arrive(w):
        def body(n):
            src, idx = other_half(w, rem4(n), lax.div(n, 4))
            wait_recv(src, wsr.at[w, idx])

        loop(1, 16, body)

    def weight_sends_done(w):
        def body1(k):
            src, idx = block(w, 0, 0)
            wait_send(src, w1s.at[w, k])

        loop(1, 4, body1)

        def body2(i):
            src, idx = block(w, i, 0)
            for k in (1, 2, 3):
                wait_send(src, w2s.at[w, i * 4 + k])

        loop(0, 4, body2)

        def body3(n):
            src, idx = block(w, rem4(n), lax.div(n, 4))
            wait_send(src, wss.at[w, idx])

        loop(1, 16, body3)

    first_send(0)
    nt_copy = rcopy(nt.at[c], nt.at[c], nts, ntr, sibling)
    nt_copy.start()
    first_arrive(0)
    second_send(0)
    first_send(1)
    first_send(2)
    second_arrive(0)
    sibling_arrive(0)

    def kv_index(dy, dz, cc):
        yy, zz = rem4(y + dy), rem4(zh + dz)
        return yy, zz, (yy * 4 + zz) * 2 + cc

    def kv_to_sibling(dy, dz):
        yy, zz, n = kv_index(dy, dz, c)
        src = kv.at[yy, zz, c]
        rcopy(src, src, kss.at[yy * 4 + zz], kvr.at[n], sibling).start()

    def kv_to_y(dz):
        yy, zz, n = kv_index(0, dz, c)
        src = kv.at[yy, zz, c]
        for k in (1, 3, 2):
            rcopy(src, src, kys.at[dz * 4 + k], kvr.at[n], at(dy=k)).start()

    def kv_arrive(dy, dz, cc):
        yy, zz, n = kv_index(dy, dz, cc)
        wait_recv(kv.at[yy, zz, cc], kvr.at[n])

    kv[y, zh, c] = mm(nrm[...], wkv[...].reshape(D, 2 * HD)).astype(BF)
    own = kv.at[y, zh, c]
    own_n = (y * 4 + zh) * 2 + c
    for k in (2, 1, 3):
        rcopy(own, own, kzs.at[k], kvr.at[own_n], at(dz=4 * k)).start()
    kv_to_y(0)
    kv_to_sibling(0, 0)

    first_arrive(1)
    second_send(1)
    first_arrive(2)
    for d in (1, 3, 2):
        kv_arrive(0, d, c)
        kv_to_y(d)
        kv_to_sibling(0, d)
    second_arrive(1)
    second_send(2)
    sibling_arrive(1)

    queries = mm(nrm[...], wq[...].reshape(D, ROWS))
    for h in range(HEADS):
        head = queries[:, h * HD : (h + 1) * HD].astype(BF)
        qs[h * TOK : (h + 1) * TOK, :] = head
        qt[:, h * TOK : (h + 1) * TOK] = head.astype(F32).T.astype(BF)

    mrow[...] = jnp.full((ROWS, 128), -1e30, F32)
    lrow[...] = jnp.zeros((ROWS, 128), F32)
    acc[...] = jnp.zeros((ROWS, HD), F32)

    def forward(k):
        yy = rem4(y + k)

        def scores(u):
            keys = kv[yy, u].reshape(256, 256)[:, :HD]
            sbuf[u] = mm_nt(qs[...], keys)

        loop(0, 4, scores)

        def rows(r):
            rs = pl.ds(pl.multiple_of(r * 64, 64), 64)
            peak = mrow[rs, :]
            new = peak
            for u in range(4):
                s = sbuf[u, rs, :]
                new = jnp.maximum(new, jnp.maximum(s[:, :128], s[:, 128:]))
            new = jnp.broadcast_to(jnp.max(new, axis=1, keepdims=True), (64, 128))
            fix = jnp.exp2((peak - new) * LOG2)
            base = new * LOG2
            total = lrow[rs, :] * fix
            for u in range(4):
                s = sbuf[u, rs, :]
                e0 = jnp.exp2(s[:, :128] * LOG2 - base)
                e1 = jnp.exp2(s[:, 128:] * LOG2 - base)
                total = total + (e0 + e1)
                ebuf[k, u, rs, :128] = e0.astype(BF)
                ebuf[k, u, rs, 128:] = e1.astype(BF)
            lrow[rs, :] = total
            mrow[rs, :] = new
            mk[k, rs, :] = new
            acc[rs, :] = acc[rs, :] * fix

        loop(0, ROWS // 64, rows)

        def values(u):
            vals = kv[yy, u].reshape(256, 256)[:, HD:]
            acc[...] += mm(ebuf[k, u], vals)

        loop(0, 4, values)

    def gather_y(k):
        for d in (0, 1, 3, 2):
            kv_arrive(k, d, c)
            kv_to_sibling(k, d)

    def sibling_y(k):
        loop(0, 4, lambda d: kv_arrive(k, d, 1 - c))

    sibling_y(0)
    forward(0)
    for k in (1, 3):
        gather_y(k)
        sibling_y(k)
        forward(k)
    gather_y(2)

    second_arrive(2)
    sibling_arrive(2)
    d_att = mm_nt(cot_ref[...], wo[...].reshape(ROWS, D)).astype(BF)
    for h in range(HEADS):
        dos[h * TOK : (h + 1) * TOK, :] = d_att[:, h * HD : (h + 1) * HD]
    sibling_y(2)
    forward(2)

    for h in range(HEADS):
        hs = slice(h * TOK, (h + 1) * TOK)
        mass = jnp.sum(lrow[hs, :], axis=1, keepdims=True)
        inv_l = jnp.broadcast_to(1.0 / mass, (TOK, 128))
        o = acc[hs, :] * inv_l
        att[:, hs] = o.astype(BF)
        top = mrow[hs, :]
        grad = dos[hs, :].astype(F32)
        for k in range(4):
            scaled = (grad * (inv_l * jnp.exp2((mk[k, hs, :] - top) * LOG2))).astype(BF)
            dog[k, hs, :] = scaled
            scaled = scaled.astype(F32)
            delta[k, hs, :] = jnp.broadcast_to(jnp.sum(scaled * o, axis=1, keepdims=True), (TOK, 128))
            dot_[k, :, hs] = scaled.T.astype(BF)

    dq[...] = jnp.zeros((ROWS, HD), F32)

    def unit(d, k):
        yy, zz = rem4(y + k), rem4(zh + d)
        block_kv = kv[yy, zz].reshape(256, 256)
        e = ebuf[k, zz]
        dp = mm_nt(dog[k], block_kv[:, HD:])
        dl = delta[k]
        ef = e.astype(F32)
        ds = jnp.concatenate(
            [ef[:, :128] * (dp[:, :128] - dl), ef[:, 128:] * (dp[:, 128:] - dl)], axis=1
        ).astype(BF)
        dq[...] += mm(ds, block_kv[:, :HD])
        part[d, k, 0] = (mm(qt[...], ds) * SCALE).astype(BF)
        part[d, k, 1] = mm(dot_[k], e).astype(BF)
        n = d * 4 + k
        rcopy(part.at[d, k, 1 - c], sib.at[d, k], rss.at[n], rsr.at[n], sibling).start()

    def to_y(d):
        def body(k):
            n = d * 4 + k
            wait_recv(sib.at[d, k], rsr.at[n])
            mine[d, k] = (part[d, k, c].astype(F32) + sib[d, k].astype(F32)).astype(BF)

        for k in (2, 1, 3):
            body(k)
            n = d * 4 + k
            rcopy(mine.at[d, k], yrec.at[d, k], rys.at[n], ryr.at[n], at(dy=k)).start()
        body(0)

    def to_z(d):
        total = mine[d, 0].astype(F32)
        for k in (1, 3, 2):
            wait_recv(yrec.at[d, k], ryr.at[d * 4 + k])
            total = total + yrec[d, k].astype(F32)
        if d == 0:
            return total
        zsum[d] = total.astype(BF)
        rcopy(zsum.at[d], zrec.at[d], rzs.at[d], rzr.at[d], at(dz=4 * d)).start()

    for n, d in enumerate(Z_ORDER):
        loop(0, 4, lambda k, d=d: unit(d, k))
        if n >= 1:
            to_y(Z_ORDER[n - 1])
        if n >= 2:
            to_z(Z_ORDER[n - 2])
    to_y(Z_ORDER[3])

    dqb = jnp.concatenate(
        [(dq[h * TOK : (h + 1) * TOK, :] * SCALE).astype(BF) for h in range(HEADS)], axis=1
    )
    to_z(Z_ORDER[2])
    out_ref[...] = (tok_ref[...].astype(F32) + mm(att[...], wo[...].reshape(ROWS, D))).astype(BF)
    dn[...] = mm_nt(dqb, wq[...].reshape(D, ROWS))
    total = to_z(Z_ORDER[3])
    for d in (1, 3, 2):
        wait_recv(zrec.at[d], rzr.at[d])
        total = total + zrec[d].astype(F32)
    for t in range(2):
        dtok[t] = total[:, t * TOK : (t + 1) * TOK].T.astype(BF)
    dkv[c] = dtok[c]
    d_copy = rcopy(dtok.at[1 - c], dkv.at[c], ds_, dr_, sibling)
    d_copy.start()

    nt_copy.wait_recv()
    grad = mm(nt[0], dtok[0]) + mm(nt[1], dtok[1])
    for zb in range(4):
        for xb in range(4):
            b = zb * 4 + xb
            dx, dz = rem4(xb - x + 4), rem4(zb - zl + 4)
            gr[dx * (1 - c) + dz * c, dz * (1 - c) + dx * c] = grad[b * 96 : (b + 1) * 96, :].astype(BF)
    for k in (1, 3, 2):
        sh = (1, 2, -1)[k - 1]
        rcopy(gr.at[k], ra.at[k], gas.at[k], gar.at[k], at(dx=k * (1 - c), dz=sh * c)).start()

    d_copy.wait_recv()
    d_unit = dn[...] + mm_nt(jnp.concatenate([dkv[0], dkv[1]], axis=1), wkv[...].reshape(D, 2 * HD))
    d_unit = d_unit * gain_ref[...]
    tok = tok_ref[...].astype(F32)
    inv = lax.rsqrt(jnp.mean(tok * tok, axis=-1, keepdims=True) + EPS)
    unit_rows = tok * inv
    ing_ref[...] = (
        inv * (d_unit - unit_rows * jnp.mean(d_unit * unit_rows, axis=-1, keepdims=True))
    ).astype(BF)

    for k in (1, 3, 2):
        wait_recv(ra.at[k], gar.at[k])
    for i in (2, 1, 3, 0):
        gb[i] = (
            (gr[0, i].astype(F32) + ra[1, i].astype(F32)) + (ra[2, i].astype(F32) + ra[3, i].astype(F32))
        ).astype(BF)
        if i:
            sh = (1, 2, -1)[i - 1]
            rcopy(gb.at[i], rb.at[i], gbs.at[i], gbr.at[i], at(dx=i * c, dz=sh * (1 - c))).start()
    for i in (1, 3, 2):
        wait_recv(rb.at[i], gbr.at[i])
    yg[y] = (
        (gb[0].astype(F32) + rb[1].astype(F32)) + (rb[2].astype(F32) + rb[3].astype(F32))
    ).astype(BF)
    for k in (2, 1, 3):
        rcopy(yg.at[y], yg.at[y], ygs.at[k], ygr.at[y], at(dy=k)).start()
    for k in (1, 3, 2):
        wait_recv(yg.at[rem4(y + k)], ygr.at[rem4(y + k)])
    zg[zh] = (
        (yg[0].astype(F32) + yg[1].astype(F32)) + (yg[2].astype(F32) + yg[3].astype(F32))
    ).astype(BF)
    for k in (2, 1, 3):
        rcopy(zg.at[zh], zg.at[zh], zgs.at[k], zgr.at[zh], at(dz=4 * k)).start()

    for w in range(3):
        weight_sends_done(w)
    nt_copy.wait_send()
    for k in (1, 2, 3):
        wait_send(own, kzs.at[k])

    def kv_sends(n):
        yy, zz = lax.div(n, 4), rem4(n)
        wait_send(kv.at[yy, zz, c], kss.at[n])

    loop(0, 16, kv_sends)
    for d in range(4):
        for k in (1, 2, 3):
            wait_send(own, kys.at[d * 4 + k])

    def part_sends(n):
        d, k = lax.div(n, 4), rem4(n)
        wait_send(part.at[d, k, 1 - c], rss.at[n])

    loop(0, 16, part_sends)
    for d in range(4):
        for k in (1, 2, 3):
            wait_send(mine.at[d, k], rys.at[d * 4 + k])
    for d in (1, 2, 3):
        wait_send(zsum.at[d], rzs.at[d])
    d_copy.wait_send()
    for k in (1, 2, 3):
        wait_send(gr.at[k], gas.at[k])
        wait_send(gb.at[k], gbs.at[k])
        wait_send(yg.at[y], ygs.at[k])

    for k in (1, 3, 2):
        wait_recv(zg.at[rem4(zh + k)], zgr.at[rem4(zh + k)])
    fin[c] = (
        (zg[0].astype(F32) + zg[1].astype(F32)) + (zg[2].astype(F32) + zg[3].astype(F32))
    ) * (1.0 / 256.0)
    f_copy = rcopy(fin.at[c], fin.at[c], fs, fr, sibling)
    f_copy.start()
    for k in (1, 2, 3):
        wait_send(zg.at[zh], zgs.at[k])
    wait_recv(fin.at[1 - c], fr)
    kvg_ref[:, :HD] = fin[0]
    kvg_ref[:, HD:] = fin[1]
    f_copy.wait_send()


def local(tokens, norm_gain, w_query, w_keyval, w_out, cotangent):
    vm = pltpu.VMEM
    dma = pltpu.SemaphoreType.DMA
    scratch = [
        vm((4, 4, 2, 48, 256), BF), vm((4, 4, 2, 48, 512), BF), vm((4, 4, 2, 16, D), BF),
        vm((TOK, D), BF), vm((2, D, TOK), BF), vm((4, 4, 2, TOK, 256), BF),
        vm((ROWS, HD), BF), vm((HD, ROWS), BF), vm((4, ROWS, 256), F32), vm((4, 4, ROWS, 256), BF),
        vm((ROWS, HD), F32), vm((ROWS, 128), F32), vm((4, ROWS, 128), F32), vm((ROWS, 128), F32),
        vm((ROWS, HD), BF), vm((4, ROWS, HD), BF), vm((4, HD, ROWS), BF), vm((4, ROWS, 128), F32),
        vm((TOK, ROWS), BF), vm((ROWS, HD), F32),
        vm((4, 4, 2, HD, 256), BF), vm((4, 4, HD, 256), BF), vm((4, 4, HD, 256), BF),
        vm((4, 4, HD, 256), BF), vm((4, HD, 256), BF), vm((4, HD, 256), BF),
        vm((2, TOK, HD), BF), vm((2, TOK, HD), BF), vm((TOK, D), F32),
        vm((4, 4, 96, HD), BF), vm((4, 4, 96, HD), BF), vm((4, 96, HD), BF), vm((4, 96, HD), BF),
        vm((4, 96, HD), BF), vm((4, 96, HD), BF), vm((2, 96, HD), F32),
        dma((3, 4)), dma((3, 16)), dma((3, 16)), dma((3, 16)), dma((3, 16)),
        dma((4,)), dma((16,)), dma((16,)), dma((32,)), dma, dma,
        dma((16,)), dma((16,)), dma((16,)), dma((16,)), dma((4,)), dma((4,)), dma, dma,
        dma((4,)), dma((4,)), dma((4,)), dma((4,)), dma((4,)), dma((4,)), dma((4,)), dma((4,)), dma, dma,
    ]
    whole = pl.BlockSpec(memory_space=pltpu.VMEM)
    layer_out, input_grad, keyval_grad = pl.pallas_call(
        kernel,
        out_shape=(
            jax.ShapeDtypeStruct((TOK, D), BF),
            jax.ShapeDtypeStruct((TOK, D), BF),
            jax.ShapeDtypeStruct((96, 2 * HD), F32),
        ),
        in_specs=[whole] * 6,
        out_specs=(whole, whole, whole),
        scratch_shapes=scratch,
        compiler_params=pltpu.CompilerParams(
            collective_id=0, has_side_effects=True, vmem_limit_bytes=50 * 2**20
        ),
        name="layer",
    )(tokens[0], norm_gain[None, :], w_query, w_keyval, w_out, cotangent[0])
    return layer_out[None], input_grad[None], keyval_grad


def solution(mesh):
    placed = (
        P("batch", "seq", None),
        P(),
        P("batch", None),
        P("batch", None),
        P("batch", None),
        P("batch", "seq", None),
    )
    return jax.shard_map(
        local,
        mesh=mesh,
        in_specs=placed,
        out_specs=(P("batch", "seq", None), P("batch", "seq", None), P("batch", None)),
        check_vma=False,
    )
```

```python
import math

import jax
import jax.numpy as jnp
from jax import lax
from jax.experimental import pallas as pl
from jax.experimental.pallas import tpu as pltpu
from jax.sharding import PartitionSpec as P

MESH = pl.DeviceIdType.MESH
BF, F32 = jnp.bfloat16, jnp.float32
EPS = 1e-06
HD, HEADS, TOK, D = 128, 4, 128, 1536
ROWS = HEADS * TOK
SCALE = 1.0 / math.sqrt(HD)
LOG2 = SCALE * math.log2(math.e)
NT_DIMS = (((1,), (1,)), ((), ()))


def mm(a, b):
    return jnp.dot(a, b, preferred_element_type=F32)


def mm_nt(a, b):
    return lax.dot_general(a, b, NT_DIMS, preferred_element_type=F32)


def rem4(v):
    return lax.rem(v, 4)


def kernel(
    tok_hbm, gain_hbm, wq_hbm, wkv_hbm, wo_hbm, cot_hbm,
    out_hbm, ing_hbm, kvg_hbm,
    tok_ref, gain_ref, cot_ref, ins, out_ref, ing_ref, kvg_ref, outs,
    wkv, wq, wo, nrm, nt, kv, qs, qt, sbuf, ebuf, acc, mrow, mk, lrow,
    dos, dog, dot_, delta, att, dq, part, sib, mine, yr1, yr2, yr3, tsum, tlow, zr1, zr2, zr3,
    dtok, dkv, dn, gr, ra, gb, rb, yg, zg, fin,
    w1s, w2s, wss, wr, wsr, kzs, kys, kss, kvr, nts, ntr,
    rss, rsr, rys, ryr, rzs, rzr, ds_, dr_, gas, gar, gbs, gbr, ygs, ygr, zgs, zgr, fs, fr,
):
    bi = lax.axis_index("batch")
    si = lax.axis_index("seq")
    zl, x = lax.div(bi, 4), rem4(bi)
    y, zh, c = lax.div(si, 8), rem4(lax.div(si, 2)), lax.rem(si, 2)

    def at(dx=0, dy=0, dz=0, dc=0):
        z = lax.rem(zh * 4 + zl + dz + 16, 16)
        return (
            rem4(z) * 4 + rem4(x + dx + 4),
            rem4(y + dy + 4) * 8 + lax.div(z, 4) * 2 + lax.rem(c + dc, 2),
        )

    sibling = at(dc=1)
    fwd, back = 1 + 2 * c, 3 - 2 * c
    sign = 1 - 2 * c

    def rcopy(src, dst, ssem, rsem, device):
        return pltpu.make_async_remote_copy(
            src_ref=src, dst_ref=dst, send_sem=ssem, recv_sem=rsem, device_id=device, device_id_type=MESH
        )

    def wait_recv(ref, rsem):
        rcopy(ref, ref, rsem, rsem, sibling).wait_recv()

    def wait_send(ref, ssem):
        rcopy(ref, ref, ssem, ssem, sibling).wait_send()

    def loop(lo, hi, body):
        def step(i, carry):
            body(i)
            return carry

        lax.fori_loop(lo, hi, step, 0)

    barrier = pltpu.get_barrier_semaphore()
    partners = [at(dc=1)]
    partners += [at(dx=k) for k in (1, 2, 3)]
    partners += [at(dy=k) for k in (1, 2, 3)]
    partners += [at(dz=k) for k in (1, -1, 2, -2, 4, -4)]
    for p in partners:
        pl.semaphore_signal(barrier, inc=1, device_id=p, device_id_type=MESH)

    loads = [
        pltpu.make_async_copy(tok_hbm, tok_ref, ins.at[0]),
        pltpu.make_async_copy(gain_hbm, gain_ref, ins.at[1]),
    ]
    for n, (w_hbm, w, h) in enumerate(((wkv_hbm, wkv, 48), (wq_hbm, wq, 48), (wo_hbm, wo, 16))):
        for half in range(2):
            loads.append(
                pltpu.make_async_copy(w_hbm.at[pl.ds(half * h, h)], w.at[zl, x, half], ins.at[2 + 2 * n + half])
            )
    loads.append(pltpu.make_async_copy(cot_hbm, cot_ref, ins.at[8]))
    for load in loads:
        load.start()
    loads[0].wait()
    loads[1].wait()

    def norm():
        tok = tok_ref[...].astype(F32)
        inv = lax.rsqrt(jnp.mean(tok * tok, axis=-1, keepdims=True) + EPS)
        normed = tok * inv * gain_ref[...][None, :]
        nrm[...] = normed.astype(BF)

    def norm_t():
        for i in range(D // 128):
            nt[c, i * 128 : (i + 1) * 128, :] = nrm[:, i * 128 : (i + 1) * 128].astype(F32).T.astype(BF)

    norm()
    norm_t()
    for load in loads[2:]:
        load.wait()
    pl.semaphore_wait(barrier, len(partners))

    one = c * 0 + 1
    zero = c * 0
    weights = ((wkv, c, 1 - c), (wq, zero, one), (wo, zero, one))

    def block(w, i, j):
        ref, ax, az = weights[w]
        zz, xx = rem4(zl + i * az + j * ax), rem4(x + i * ax + j * az)
        return ref.at[zz, xx, c], zz * 4 + xx

    def other_half(w, i, j):
        ref, ax, az = weights[w]
        zz, xx = rem4(zl + i * az + j * ax), rem4(x + i * ax + j * az)
        return ref.at[zz, xx, 1 - c], zz * 4 + xx

    def zshift(k):
        return rem4(k + 1) - 1

    def first_send(w):
        ref, ax, az = weights[w]

        def body(k):
            src, idx = block(w, 0, 0)
            rcopy(src, src, w1s.at[w, k], wr.at[w, idx], at(dx=k * ax, dz=zshift(k) * az)).start()

        loop(1, 4, body)

    def to_sibling(w, i, j):
        src, idx = block(w, i, j)
        rcopy(src, src, wss.at[w, idx], wsr.at[w, idx], sibling).start()

    def first_arrive(w):
        def body(i):
            src, idx = block(w, i, 0)
            wait_recv(src, wr.at[w, idx])

        loop(1, 4, body)

    def second_send(w):
        ref, ax, az = weights[w]

        def body(i):
            src, idx = block(w, i, 0)
            for k in (1, 3, 2):
                rcopy(src, src, w2s.at[w, i * 4 + k], wr.at[w, idx], at(dx=k * az, dz=zshift(k) * ax)).start()

        loop(0, 4, body)
        loop(1, 4, lambda i: to_sibling(w, i, 0))

    def second_arrive(w):
        for j in (1, 3, 2):

            def body(i, j=j):
                src, idx = block(w, i, j)
                wait_recv(src, wr.at[w, idx])
                to_sibling(w, i, j)

            loop(0, 4, body)

    def sibling_arrive(w):
        def body(n):
            src, idx = other_half(w, rem4(n), lax.div(n, 4))
            wait_recv(src, wsr.at[w, idx])

        loop(1, 16, body)

    def weight_sends_done(w):
        def body1(k):
            src, idx = block(w, 0, 0)
            wait_send(src, w1s.at[w, k])

        loop(1, 4, body1)

        def body2(i):
            src, idx = block(w, i, 0)
            for k in (1, 2, 3):
                wait_send(src, w2s.at[w, i * 4 + k])

        loop(0, 4, body2)

        def body3(n):
            src, idx = block(w, rem4(n), lax.div(n, 4))
            wait_send(src, wss.at[w, idx])

        loop(1, 16, body3)

    def ring1_send(w):
        src, idx = block(w, 0, 0)
        for n, step in ((1, 1), (2, -1)):
            rcopy(src, src, w1s.at[w, n], wr.at[w, idx], at(dz=step)).start()

    def ring1_forward(w):
        src, idx = block(w, back, 0)
        wait_recv(src, wr.at[w, idx])
        rcopy(src, src, w1s.at[w, 3], wr.at[w, idx], at(dz=sign)).start()

    def ring1_rest(w):
        for i in (fwd, 2):
            src, idx = block(w, i, 0)
            wait_recv(src, wr.at[w, idx])

    def ring2_send(w):
        def body(i):
            src, idx = block(w, i, 0)
            for n, step in ((1, 1), (2, -1)):
                rcopy(src, src, w2s.at[w, i * 4 + n], wr.at[w, idx], at(dx=step)).start()

        loop(0, 4, body)
        loop(1, 4, lambda i: to_sibling(w, i, 0))

    def ring2_forward(w):
        def body(i):
            src, idx = block(w, i, back)
            wait_recv(src, wr.at[w, idx])
            rcopy(src, src, w2s.at[w, i * 4 + 3], wr.at[w, idx], at(dx=sign)).start()
            to_sibling(w, i, back)

        loop(0, 4, body)

    def ring2_rest(w):
        for j in (fwd, 2):

            def body(i, j=j):
                src, idx = block(w, i, j)
                wait_recv(src, wr.at[w, idx])
                to_sibling(w, i, j)

            loop(0, 4, body)

    first_send(0)
    nt_copy = rcopy(nt.at[c], nt.at[c], nts, ntr, sibling)
    nt_copy.start()
    ring1_send(1)
    first_arrive(0)
    second_send(0)
    ring1_forward(1)
    ring1_send(2)
    second_arrive(0)
    ring1_rest(1)
    ring2_send(1)
    sibling_arrive(0)

    def kv_index(dy, dz, cc):
        yy, zz = rem4(y + dy), rem4(zh + dz)
        return yy, zz, (yy * 4 + zz) * 2 + cc

    def kv_to_sibling(dy, dz):
        yy, zz, n = kv_index(dy, dz, c)
        src = kv.at[yy, zz, c]
        rcopy(src, src, kss.at[yy * 4 + zz], kvr.at[2 * n], sibling).start()

    def y_send(dz, direct=False):
        yy, zz, n = kv_index(0, dz, c)
        src = kv.at[yy, zz, c]
        for k, step in ((3, 2), (1, 1), (2, -1)) if direct else ((1, 1), (2, -1)):
            rcopy(src, src, kys.at[dz * 4 + k], kvr.at[2 * n], at(dy=step)).start()
        kv_to_sibling(0, dz)

    def kv_arrive(dy, dz, cc):
        yy, zz, n = kv_index(dy, dz, cc)
        wait_recv(kv.at[yy, zz, cc], kvr.at[2 * n])

    def y_forward(dz):
        kv_arrive(back, dz, c)
        yy, zz, n = kv_index(back, dz, c)
        src = kv.at[yy, zz, c]
        rcopy(src, src, kys.at[dz * 4 + 3], kvr.at[2 * n], at(dy=sign)).start()
        kv_to_sibling(back, dz)

    def y_rest(dz, direct=False):
        for k in (back, fwd, 2) if direct else (fwd, 2):
            kv_arrive(k, dz, c)
            kv_to_sibling(k, dz)

    def y_sibling(dz):
        loop(0, 4, lambda k: kv_arrive(k, dz, 1 - c))

    def z_send(dz, half, sem, step):
        yy, zz, n = kv_index(0, dz, c)
        src = kv.at[yy, zz, c, half]
        rcopy(src, src, kzs.at[sem], kvr.at[2 * n + half], at(dz=step)).start()

    def z_arrive(dz, half):
        yy, zz, n = kv_index(0, dz, c)
        wait_recv(kv.at[yy, zz, c, half], kvr.at[2 * n + half])

    kv[y, zh, c] = mm(nrm[...], wkv[...].reshape(D, 2 * HD)).astype(BF).reshape(2, 64, 2 * HD)
    own = kv.at[y, zh, c]
    own_half = kv.at[y, zh, c, 0]
    for half in range(2):
        z_send(0, half, half, 4 * sign)
    y_send(0)
    ring1_forward(2)
    ring2_forward(1)
    y_forward(0)
    for half in range(2):
        wait_send(own_half, kzs.at[half])
    for half in range(2):
        z_send(0, half, 2 + half, -4 * sign)
    for half in range(2):
        z_arrive(back, half)
        z_send(back, half, 4 + half, 4 * sign)
    y_send(back)
    y_rest(0)
    ring1_rest(2)
    ring2_send(2)
    ring2_rest(1)
    for half in range(2):
        z_arrive(fwd, half)
    y_send(fwd)
    y_forward(back)
    sibling_arrive(1)

    def make_queries():
        queries = mm(nrm[...], wq[...].reshape(D, ROWS))
        for h in range(HEADS):
            head = queries[:, h * HD : (h + 1) * HD].astype(BF)
            qs[h * TOK : (h + 1) * TOK, :] = head
            qt[:, h * TOK : (h + 1) * TOK] = head.astype(F32).T.astype(BF)

    make_queries()

    mrow[...] = jnp.full((ROWS, 128), -1e30, F32)
    lrow[...] = jnp.zeros((ROWS, 128), F32)
    acc[...] = jnp.zeros((ROWS, HD), F32)

    def forward(k):
        zz = rem4(zh + k)

        def scores():
            for u in range(4):
                keys = kv[u, zz].reshape(256, 256)[:, :HD]
                sbuf[u] = mm_nt(qs[...], keys)

        scores()

        def rows(start, count):
            rs = pl.ds(start, count)
            peak = mrow[rs, :]
            new = peak
            for u in range(4):
                s = sbuf[u, rs, :]
                new = jnp.maximum(new, jnp.maximum(s[:, :128], s[:, 128:]))
            new = jnp.broadcast_to(jnp.max(new, axis=1, keepdims=True), (count, 128))
            fix = jnp.exp2((peak - new) * LOG2)
            base = new * LOG2
            total = lrow[rs, :] * fix
            for u in range(4):
                s = sbuf[u, rs, :]
                e0 = jnp.exp2(s[:, :128] * LOG2 - base)
                e1 = jnp.exp2(s[:, 128:] * LOG2 - base)
                total = total + (e0 + e1)
                ebuf[k, u, rs, :128] = e0.astype(BF)
                ebuf[k, u, rs, 128:] = e1.astype(BF)
            lrow[rs, :] = total
            mrow[rs, :] = new
            mk[k, rs, :] = new
            acc[rs, :] = acc[rs, :] * fix

        def all_rows(r):
            for part_of in range(4):
                rows(pl.multiple_of(r * 128 + part_of * 32, 32), 32)

        loop(0, 4, all_rows)

        def values():
            total = acc[...]
            for u in range(4):
                total = total + mm(ebuf[k, u], kv[u, zz].reshape(256, 256)[:, HD:])
            acc[...] = total

        values()

    y_sibling(0)
    forward(0)
    y_forward(fwd)
    ring2_forward(2)
    for half in range(2):
        z_arrive(2, half)
    y_send(2, direct=True)
    y_rest(back)
    y_rest(fwd)
    y_sibling(1)
    forward(1)
    ring2_rest(2)
    y_sibling(3)
    forward(3)
    y_rest(2, direct=True)
    sibling_arrive(2)

    def make_d_att():
        d_att = mm_nt(cot_ref[...], wo[...].reshape(ROWS, D)).astype(BF)
        for h in range(HEADS):
            dos[h * TOK : (h + 1) * TOK, :] = d_att[:, h * HD : (h + 1) * HD]

    make_d_att()
    y_sibling(2)
    forward(2)

    def per_row():
        for h in range(HEADS):
            hs = slice(h * TOK, (h + 1) * TOK)
            mass = jnp.sum(lrow[hs, :], axis=1, keepdims=True)
            inv_l = jnp.broadcast_to(1.0 / mass, (TOK, 128))
            o = acc[hs, :] * inv_l
            att[:, hs] = o.astype(BF)
            top = mrow[hs, :]
            grad = dos[hs, :].astype(F32)
            for k in range(4):
                scaled = (grad * (inv_l * jnp.exp2((mk[k, hs, :] - top) * LOG2))).astype(BF)
                dog[k, hs, :] = scaled
                scaled = scaled.astype(F32)
                delta[k, hs, :] = jnp.broadcast_to(jnp.sum(scaled * o, axis=1, keepdims=True), (TOK, 128))
                dot_[k, :, hs] = scaled.T.astype(BF)

    per_row()

    dq[...] = jnp.zeros((ROWS, HD), F32)

    def unit(d, k):
        unit_compute(d, k)
        n = d * 4 + k
        rcopy(part.at[d, k, 1 - c], sib.at[d, k], rss.at[n], rsr.at[n], sibling).start()

    def unit_compute(d, k):
        yy, zz = rem4(y + k), rem4(zh + d)
        block_kv = kv[yy, zz].reshape(256, 256)
        e = ebuf[d, yy]
        dp = mm_nt(dog[d], block_kv[:, HD:])
        dl = delta[d]
        ef = e.astype(F32)
        ds = jnp.concatenate(
            [ef[:, :128] * (dp[:, :128] - dl), ef[:, 128:] * (dp[:, 128:] - dl)], axis=1
        ).astype(BF)
        dq[...] += mm(ds, block_kv[:, :HD])
        part[d, k, 0] = (mm(qt[...], ds) * SCALE).astype(BF)
        part[d, k, 1] = mm(dot_[d], e).astype(BF)

    def own_half_of(d, k):
        wait_recv(sib.at[d, k], rsr.at[d * 4 + k])
        return part[d, k, c].astype(F32) + sib[d, k].astype(F32)

    def y_out(d):
        mine[d, 2] = own_half_of(d, 2).astype(BF)
        rcopy(mine.at[d, 2], yr1.at[d], rys.at[d * 4 + 1], ryr.at[d * 4 + 1], at(dy=sign)).start()
        mine[d, back] = own_half_of(d, back).astype(BF)
        rcopy(mine.at[d, back], yr2.at[d], rys.at[d * 4 + 2], ryr.at[d * 4 + 2], at(dy=-sign)).start()

    def y_add(d):
        total = own_half_of(d, fwd)
        wait_recv(yr1.at[d], ryr.at[d * 4 + 1])
        mine[d, fwd] = (total + yr1[d].astype(F32)).astype(BF)
        rcopy(mine.at[d, fwd], yr3.at[d], rys.at[d * 4 + 3], ryr.at[d * 4 + 3], at(dy=sign)).start()

    def y_total(d):
        total = own_half_of(d, 0)
        wait_recv(yr2.at[d], ryr.at[d * 4 + 2])
        wait_recv(yr3.at[d], ryr.at[d * 4 + 3])
        return total + (yr2[d].astype(F32) + yr3[d].astype(F32))

    def y_out_direct(d):
        for k, dst in ((2, yr2), (1, yr1), (3, yr3)):
            mine[d, k] = own_half_of(d, k).astype(BF)
            n = d * 4 + k
            rcopy(mine.at[d, k], dst.at[d], rys.at[n], ryr.at[n], at(dy=k)).start()

    def y_total_direct(d):
        total = own_half_of(d, 0)
        for k, src in ((1, yr1), (3, yr3), (2, yr2)):
            wait_recv(src.at[d], ryr.at[d * 4 + k])
            total = total + src[d].astype(F32)
        return total

    def z_out(src, dst, sem, step):
        rcopy(src, dst, rzs.at[sem], rzr.at[sem], at(dz=step)).start()

    def batch(d):
        for k in (2, 1, 3, 0):
            unit(d, k)

    batch(2)
    y_out_direct(2)
    batch(1)
    y_out(1)
    tlow[2] = y_total_direct(2).astype(BF).reshape(2, 64, 256)
    for half in range(2):
        z_out(tlow.at[2, half], zr1.at[half], half, 4 * sign)
    batch(3)
    y_add(1)
    y_out(3)
    batch(0)
    tsum[1] = y_total(1)
    y_add(3)
    y_out(0)
    tsum[3] = y_total(3)
    tlow[back] = tsum[back].astype(BF).reshape(2, 64, 256)
    z_out(tlow.at[back], zr2, 2, -4 * sign)
    y_add(0)
    for half in range(2):
        wait_recv(zr1.at[half], rzr.at[half])
        tlow[fwd, half] = (tsum[fwd, half * 64 : (half + 1) * 64, :] + zr1[half].astype(F32)).astype(BF)
        z_out(tlow.at[fwd, half], zr3.at[half], 3 + half, 4 * sign)

    def make_dn():
        dqb = jnp.concatenate(
            [(dq[h * TOK : (h + 1) * TOK, :] * SCALE).astype(BF) for h in range(HEADS)], axis=1
        )
        dn[...] = mm_nt(dqb, wq[...].reshape(D, ROWS))

    out_ref[...] = (tok_ref[...].astype(F32) + mm(att[...], wo[...].reshape(ROWS, D))).astype(BF)
    out_copy = pltpu.make_async_copy(out_ref, out_hbm, outs.at[0])
    out_copy.start()
    make_dn()
    total = y_total(0)
    wait_recv(zr2, rzr.at[2])
    for half in range(2):
        wait_recv(zr3.at[half], rzr.at[3 + half])
    total = total + (zr2[...].reshape(128, 256).astype(F32) + zr3[...].reshape(128, 256).astype(F32))
    for t in range(2):
        dtok[t] = total[:, t * TOK : (t + 1) * TOK].T.astype(BF)
    dkv[c] = dtok[c]
    d_copy = rcopy(dtok.at[1 - c], dkv.at[c], ds_, dr_, sibling)
    d_copy.start()

    nt_copy.wait_recv()
    def make_grad():
        grad = mm(nt[0], dtok[0]) + mm(nt[1], dtok[1])
        for zb in range(4):
            for xb in range(4):
                b = zb * 4 + xb
                dx, dz = rem4(xb - x + 4), rem4(zb - zl + 4)
                gr[dx * (1 - c) + dz * c, dz * (1 - c) + dx * c] = grad[b * 96 : (b + 1) * 96, :].astype(BF)

    make_grad()
    for k in (1, 3, 2):
        sh = (1, 2, -1)[k - 1]
        rcopy(gr.at[k], ra.at[k], gas.at[k], gar.at[k], at(dx=k * (1 - c), dz=sh * c)).start()

    d_copy.wait_recv()
    def make_input_grad():
        d_unit = dn[...] + mm_nt(jnp.concatenate([dkv[0], dkv[1]], axis=1), wkv[...].reshape(D, 2 * HD))
        d_unit = d_unit * gain_ref[...][None, :]
        tok = tok_ref[...].astype(F32)
        inv = lax.rsqrt(jnp.mean(tok * tok, axis=-1, keepdims=True) + EPS)
        unit_rows = tok * inv
        ing_ref[...] = (
            inv * (d_unit - unit_rows * jnp.mean(d_unit * unit_rows, axis=-1, keepdims=True))
        ).astype(BF)

    make_input_grad()
    ing_copy = pltpu.make_async_copy(ing_ref, ing_hbm, outs.at[1])
    ing_copy.start()

    for k in (1, 3, 2):
        wait_recv(ra.at[k], gar.at[k])
    for i in (2, 1, 3, 0):
        gb[i] = (
            (gr[0, i].astype(F32) + ra[1, i].astype(F32)) + (ra[2, i].astype(F32) + ra[3, i].astype(F32))
        ).astype(BF)
        if i:
            sh = (1, 2, -1)[i - 1]
            rcopy(gb.at[i], rb.at[i], gbs.at[i], gbr.at[i], at(dx=i * c, dz=sh * (1 - c))).start()
    for i in (1, 3, 2):
        wait_recv(rb.at[i], gbr.at[i])
    yg[y] = (
        (gb[0].astype(F32) + rb[1].astype(F32)) + (rb[2].astype(F32) + rb[3].astype(F32))
    ).astype(BF)
    for k in (2, 1, 3):
        rcopy(yg.at[y], yg.at[y], ygs.at[k], ygr.at[y], at(dy=k)).start()
    for k in (1, 3, 2):
        wait_recv(yg.at[rem4(y + k)], ygr.at[rem4(y + k)])
    zg[zh] = (
        (yg[0].astype(F32) + yg[1].astype(F32)) + (yg[2].astype(F32) + yg[3].astype(F32))
    ).astype(BF)
    for k, step in ((2, 8), (1, 4), (3, -4)):
        rcopy(zg.at[zh], zg.at[zh], zgs.at[k], zgr.at[zh], at(dz=step)).start()

    for w in range(3):
        weight_sends_done(w)
    nt_copy.wait_send()
    for n in range(2, 6):
        wait_send(own_half, kzs.at[n])

    def kv_sends(n):
        yy, zz = lax.div(n, 4), rem4(n)
        wait_send(kv.at[yy, zz, c], kss.at[n])

    loop(0, 16, kv_sends)
    for d in range(4):
        for k in (1, 2, 3):
            wait_send(own, kys.at[d * 4 + k])

    def part_sends(n):
        d, k = lax.div(n, 4), rem4(n)
        wait_send(part.at[d, k, 1 - c], rss.at[n])

    loop(0, 16, part_sends)
    for d in range(4):
        for k in (1, 2, 3):
            wait_send(mine.at[d, k], rys.at[d * 4 + k])
    for n in (0, 1, 3, 4):
        wait_send(zr1.at[0], rzs.at[n])
    wait_send(zr2, rzs.at[2])
    d_copy.wait_send()
    for k in (1, 2, 3):
        wait_send(gr.at[k], gas.at[k])
        wait_send(gb.at[k], gbs.at[k])
        wait_send(yg.at[y], ygs.at[k])

    for k in (1, 3, 2):
        wait_recv(zg.at[rem4(zh + k)], zgr.at[rem4(zh + k)])
    fin[c] = (
        (zg[0].astype(F32) + zg[1].astype(F32)) + (zg[2].astype(F32) + zg[3].astype(F32))
    ) * (1.0 / 256.0)
    f_copy = rcopy(fin.at[c], fin.at[c], fs, fr, sibling)
    f_copy.start()
    for k in (1, 2, 3):
        wait_send(zg.at[zh], zgs.at[k])
    wait_recv(fin.at[1 - c], fr)
    kvg_ref[:, :HD] = fin[0]
    kvg_ref[:, HD:] = fin[1]
    kvg_copy = pltpu.make_async_copy(kvg_ref, kvg_hbm, outs.at[2])
    kvg_copy.start()
    out_copy.wait()
    ing_copy.wait()
    kvg_copy.wait()
    f_copy.wait_send()


def hand_over(a, b, d, a_out, b_out, d_out, a_buf, b_buf, d_buf, sems):
    moves = ((a, a_buf, a_out), (b, b_buf, b_out), (d, d_buf, d_out))
    reads = [pltpu.make_async_copy(src, buf, sems.at[n]) for n, (src, buf, dst) in enumerate(moves)]
    writes = [pltpu.make_async_copy(buf, dst, sems.at[3 + n]) for n, (src, buf, dst) in enumerate(moves)]
    for copy in reads:
        copy.start()
    for read, write in zip(reads, writes):
        read.wait()
        write.start()
    for copy in writes:
        copy.wait()


def local(tokens, norm_gain, w_query, w_keyval, w_out, cotangent):
    vm = pltpu.VMEM
    dma = pltpu.SemaphoreType.DMA
    scratch = [
        vm((TOK, D), BF), vm((D,), F32), vm((TOK, D), BF), dma((9,)),
        vm((TOK, D), BF), vm((TOK, D), BF), vm((96, 2 * HD), F32), dma((3,)),
        vm((4, 4, 2, 48, 256), BF), vm((4, 4, 2, 48, 512), BF), vm((4, 4, 2, 16, D), BF),
        vm((TOK, D), BF), vm((2, D, TOK), BF), vm((4, 4, 2, 2, 64, 256), BF),
        vm((ROWS, HD), BF), vm((HD, ROWS), BF), vm((4, ROWS, 256), F32), vm((4, 4, ROWS, 256), BF),
        vm((ROWS, HD), F32), vm((ROWS, 128), F32), vm((4, ROWS, 128), F32), vm((ROWS, 128), F32),
        vm((ROWS, HD), BF), vm((4, ROWS, HD), BF), vm((4, HD, ROWS), BF), vm((4, ROWS, 128), F32),
        vm((TOK, ROWS), BF), vm((ROWS, HD), F32),
        vm((4, 4, 2, HD, 256), BF), vm((4, 4, HD, 256), BF), vm((4, 4, HD, 256), BF),
        vm((4, HD, 256), BF), vm((4, HD, 256), BF), vm((4, HD, 256), BF),
        vm((4, HD, 256), F32), vm((4, 2, 64, 256), BF),
        vm((2, 64, 256), BF), vm((2, 64, 256), BF), vm((2, 64, 256), BF),
        vm((2, TOK, HD), BF), vm((2, TOK, HD), BF), vm((TOK, D), F32),
        vm((4, 4, 96, HD), BF), vm((4, 4, 96, HD), BF), vm((4, 96, HD), BF), vm((4, 96, HD), BF),
        vm((4, 96, HD), BF), vm((4, 96, HD), BF), vm((2, 96, HD), F32),
        dma((3, 4)), dma((3, 16)), dma((3, 16)), dma((3, 16)), dma((3, 16)),
        dma((6,)), dma((16,)), dma((16,)), dma((64,)), dma, dma,
        dma((16,)), dma((16,)), dma((16,)), dma((16,)), dma((5,)), dma((5,)), dma, dma,
        dma((4,)), dma((4,)), dma((4,)), dma((4,)), dma((4,)), dma((4,)), dma((4,)), dma((4,)), dma, dma,
    ]
    hbm = pl.BlockSpec(memory_space=pltpu.HBM)
    shapes = (
        jax.ShapeDtypeStruct((TOK, D), BF),
        jax.ShapeDtypeStruct((TOK, D), BF),
        jax.ShapeDtypeStruct((96, 2 * HD), F32),
    )
    results = pl.pallas_call(
        kernel,
        out_shape=shapes,
        in_specs=[hbm] * 6,
        out_specs=(hbm, hbm, hbm),
        scratch_shapes=scratch,
        compiler_params=pltpu.CompilerParams(
            collective_id=0, has_side_effects=True, vmem_limit_bytes=63 * 2**20
        ),
        name="layer",
    )(tokens[0], norm_gain, w_query, w_keyval, w_out, cotangent[0])
    layer_out, input_grad, keyval_grad = pl.pallas_call(
        hand_over,
        out_shape=shapes,
        in_specs=[hbm] * 3,
        out_specs=(hbm, hbm, hbm),
        scratch_shapes=[vm((TOK, D), BF), vm((TOK, D), BF), vm((96, 2 * HD), F32), dma((6,))],
        compiler_params=pltpu.CompilerParams(vmem_limit_bytes=63 * 2**20),
        name="hand_over",
    )(*results)
    return layer_out[None], input_grad[None], keyval_grad


def solution(mesh):
    placed = (
        P("batch", "seq", None),
        P(),
        P("batch", None),
        P("batch", None),
        P("batch", None),
        P("batch", "seq", None),
    )
    return jax.shard_map(
        local,
        mesh=mesh,
        in_specs=placed,
        out_specs=(P("batch", "seq", None), P("batch", "seq", None), P("batch", None)),
        check_vma=False,
    )
```

```python
import math

import jax
import jax.numpy as jnp
from jax import lax
from jax.experimental import pallas as pl
from jax.experimental.pallas import tpu as pltpu
from jax.sharding import PartitionSpec as P

MESH = pl.DeviceIdType.MESH
BF, F32 = jnp.bfloat16, jnp.float32
EPS = 1e-06
HD, HEADS, TOK, D = 128, 4, 128, 1536
ROWS = HEADS * TOK
SCALE = 1.0 / math.sqrt(HD)
LOG2 = SCALE * math.log2(math.e)
NT_DIMS = (((1,), (1,)), ((), ()))


def mm(a, b):
    return jnp.dot(a, b, preferred_element_type=F32)


def mm_nt(a, b):
    return lax.dot_general(a, b, NT_DIMS, preferred_element_type=F32)


def rem4(v):
    return lax.rem(v, 4)


def kernel(
    tok_hbm, gain_hbm, wq_hbm, wkv_hbm, wo_hbm, cot_hbm,
    out_hbm, ing_hbm, kvg_hbm,
    tok_ref, gain_ref, cot_ref, ins, out_ref, ing_ref, kvg_ref, outs,
    wk, wv, wq, wo, nrm, nt, kv, qs, qt, sbuf, ebuf, acc, mrow, mk, lrow,
    dos, dog, dot_, delta, att, dq, part, sib, mine, yr1, yr2, yr3, tsum, tlow, zr1, zr2, zr3,
    dtok, dkv, dn, gr, ra, gb, rb, yg, zg, fin,
    w1s, w2s, wss, wr, wsr, kzs, kys, kss, kvr, nts, ntr,
    rss, rsr, rys, ryr, rzs, rzr, ds_, dr_, gas, gar, gbs, gbr, ygs, ygr, zgs, zgr, fs, fr,
):
    bi = lax.axis_index("batch")
    si = lax.axis_index("seq")
    zl, x = lax.div(bi, 4), rem4(bi)
    y, zh, c = lax.div(si, 8), rem4(lax.div(si, 2)), lax.rem(si, 2)

    def at(dx=0, dy=0, dz=0, dc=0):
        z = lax.rem(zh * 4 + zl + dz + 16, 16)
        return (
            rem4(z) * 4 + rem4(x + dx + 4),
            rem4(y + dy + 4) * 8 + lax.div(z, 4) * 2 + lax.rem(c + dc, 2),
        )

    sibling = at(dc=1)
    fwd, back = 1 + 2 * c, 3 - 2 * c
    sign = 1 - 2 * c

    def rcopy(src, dst, ssem, rsem, device):
        return pltpu.make_async_remote_copy(
            src_ref=src, dst_ref=dst, send_sem=ssem, recv_sem=rsem, device_id=device, device_id_type=MESH
        )

    def wait_recv(ref, rsem):
        rcopy(ref, ref, rsem, rsem, sibling).wait_recv()

    def wait_send(ref, ssem):
        rcopy(ref, ref, ssem, ssem, sibling).wait_send()

    def loop(lo, hi, body):
        def step(i, carry):
            body(i)
            return carry

        lax.fori_loop(lo, hi, step, 0)

    barrier = pltpu.get_barrier_semaphore()
    partners = [at(dc=1)]
    partners += [at(dx=k) for k in (1, 2, 3)]
    partners += [at(dy=k) for k in (1, 2, 3)]
    partners += [at(dz=k) for k in (1, -1, 2, -2, 4, -4)]
    for p in partners:
        pl.semaphore_signal(barrier, inc=1, device_id=p, device_id_type=MESH)

    loads = [
        pltpu.make_async_copy(tok_hbm, tok_ref, ins.at[0]),
        pltpu.make_async_copy(gain_hbm, gain_ref, ins.at[1]),
    ]
    own_parts = ((wkv_hbm, wk, 48, 0, HD), (wkv_hbm, wv, 48, HD, HD), (wq_hbm, wq, 48, 0, ROWS), (wo_hbm, wo, 16, 0, D))
    for n, (w_hbm, w, h, col, width) in enumerate(own_parts):
        for half in range(2):
            src = w_hbm.at[pl.ds(half * h, h), pl.ds(col, width)]
            loads.append(pltpu.make_async_copy(src, w.at[zl, x, half], ins.at[2 + 2 * n + half]))
    loads.append(pltpu.make_async_copy(cot_hbm, cot_ref, ins.at[10]))
    for load in loads:
        load.start()
    loads[0].wait()
    loads[1].wait()

    def norm():
        tok = tok_ref[...].astype(F32)
        inv = lax.rsqrt(jnp.mean(tok * tok, axis=-1, keepdims=True) + EPS)
        normed = tok * inv * gain_ref[...][None, :]
        nrm[...] = normed.astype(BF)

    def norm_t():
        for i in range(D // 128):
            nt[c, i * 128 : (i + 1) * 128, :] = nrm[:, i * 128 : (i + 1) * 128].astype(F32).T.astype(BF)

    norm()
    norm_t()
    for load in loads[2:]:
        load.wait()
    pl.semaphore_wait(barrier, len(partners))

    one = c * 0 + 1
    zero = c * 0
    weights = ((wk, c, 1 - c), (wq, zero, one), (wo, zero, one), (wv, c, 1 - c))

    def block(w, i, j):
        ref, ax, az = weights[w]
        zz, xx = rem4(zl + i * az + j * ax), rem4(x + i * ax + j * az)
        return ref.at[zz, xx, c], zz * 4 + xx

    def other_half(w, i, j):
        ref, ax, az = weights[w]
        zz, xx = rem4(zl + i * az + j * ax), rem4(x + i * ax + j * az)
        return ref.at[zz, xx, 1 - c], zz * 4 + xx

    def zshift(k):
        return rem4(k + 1) - 1

    def first_send(w):
        ref, ax, az = weights[w]

        def body(k):
            src, idx = block(w, 0, 0)
            rcopy(src, src, w1s.at[w, k], wr.at[w, idx], at(dx=k * ax, dz=zshift(k) * az)).start()

        loop(1, 4, body)

    def to_sibling(w, i, j):
        src, idx = block(w, i, j)
        rcopy(src, src, wss.at[w, idx], wsr.at[w, idx], sibling).start()

    def first_arrive(w):
        def body(i):
            src, idx = block(w, i, 0)
            wait_recv(src, wr.at[w, idx])

        loop(1, 4, body)

    def second_send(w):
        ref, ax, az = weights[w]

        def body(i):
            src, idx = block(w, i, 0)
            for k in (1, 3, 2):
                rcopy(src, src, w2s.at[w, i * 4 + k], wr.at[w, idx], at(dx=k * az, dz=zshift(k) * ax)).start()

        loop(0, 4, body)
        loop(1, 4, lambda i: to_sibling(w, i, 0))

    def second_arrive(w):
        for j in (1, 3, 2):

            def body(i, j=j):
                src, idx = block(w, i, j)
                wait_recv(src, wr.at[w, idx])
                to_sibling(w, i, j)

            loop(0, 4, body)

    def sibling_arrive(w):
        def body(n):
            src, idx = other_half(w, rem4(n), lax.div(n, 4))
            wait_recv(src, wsr.at[w, idx])

        loop(1, 16, body)

    def weight_sends_done(w):
        def body1(k):
            src, idx = block(w, 0, 0)
            wait_send(src, w1s.at[w, k])

        loop(1, 4, body1)

        def body2(i):
            src, idx = block(w, i, 0)
            for k in (1, 2, 3):
                wait_send(src, w2s.at[w, i * 4 + k])

        loop(0, 4, body2)

        def body3(n):
            src, idx = block(w, rem4(n), lax.div(n, 4))
            wait_send(src, wss.at[w, idx])

        loop(1, 16, body3)

    def ring1_send(w):
        src, idx = block(w, 0, 0)
        for n, step in ((1, 1), (2, -1)):
            rcopy(src, src, w1s.at[w, n], wr.at[w, idx], at(dz=step)).start()

    def ring1_forward(w):
        src, idx = block(w, back, 0)
        wait_recv(src, wr.at[w, idx])
        rcopy(src, src, w1s.at[w, 3], wr.at[w, idx], at(dz=sign)).start()

    def ring1_rest(w):
        for i in (fwd, 2):
            src, idx = block(w, i, 0)
            wait_recv(src, wr.at[w, idx])

    def ring2_send(w):
        def body(i):
            src, idx = block(w, i, 0)
            for n, step in ((1, 1), (2, -1)):
                rcopy(src, src, w2s.at[w, i * 4 + n], wr.at[w, idx], at(dx=step)).start()

        loop(0, 4, body)
        loop(1, 4, lambda i: to_sibling(w, i, 0))

    def ring2_forward(w):
        def body(i):
            src, idx = block(w, i, back)
            wait_recv(src, wr.at[w, idx])
            rcopy(src, src, w2s.at[w, i * 4 + 3], wr.at[w, idx], at(dx=sign)).start()
            to_sibling(w, i, back)

        loop(0, 4, body)

    def ring2_rest(w):
        for j in (fwd, 2):

            def body(i, j=j):
                src, idx = block(w, i, j)
                wait_recv(src, wr.at[w, idx])
                to_sibling(w, i, j)

            loop(0, 4, body)

    first_send(0)
    first_send(3)
    ring1_send(1)
    first_arrive(0)
    second_send(0)
    first_arrive(3)
    second_send(3)
    nt_copy = rcopy(nt.at[c], nt.at[c], nts, ntr, sibling)
    nt_copy.start()
    ring1_forward(1)
    ring1_send(2)
    second_arrive(0)

    def kv_index(dy, dz, cc):
        yy, zz = rem4(y + dy), rem4(zh + dz)
        return yy, zz, (yy * 4 + zz) * 2 + cc

    def kv_to_sibling(dy, dz):
        yy, zz, n = kv_index(dy, dz, c)
        src = kv.at[yy, zz, c]
        rcopy(src, src, kss.at[dy * 4 + dz], kvr.at[2 * n], sibling).start()

    def half_to_sibling(dy, half):
        yy, zz, n = kv_index(dy, 2, c)
        src = kv.at[yy, zz, c, half]
        rcopy(src, src, kss.at[dy * 4 + 2 + half * (14 - 3 * dy)], kvr.at[2 * n + half], sibling).start()

    def half_arrive(dy, half, cc):
        yy, zz, n = kv_index(dy, 2, cc)
        wait_recv(kv.at[yy, zz, cc, half], kvr.at[2 * n + half])

    def far_send(half):
        yy, zz, n = kv_index(0, 2, c)
        src = kv.at[yy, zz, c, half]
        half_arrive(0, half, c)
        for k, step in ((3, 2), (1, 1), (2, -1)):
            rcopy(src, src, kys.at[8 + k + half * 8], kvr.at[2 * n + half], at(dy=step)).start()
        half_to_sibling(0, half)

    def far_rest(half):
        for dy in (1, 3, 2):
            half_arrive(dy, half, c)
            half_to_sibling(dy, half)

    def far_sibling():
        for half in range(2):
            for dy in range(4):
                half_arrive(dy, half, 1 - c)

    def y_send(dz):
        yy, zz, n = kv_index(0, dz, c)
        src = kv.at[yy, zz, c]
        for k, step in ((1, 1), (2, -1)):
            rcopy(src, src, kys.at[dz * 4 + k], kvr.at[2 * n], at(dy=step)).start()
        kv_to_sibling(0, dz)

    def kv_arrive(dy, dz, cc):
        yy, zz, n = kv_index(dy, dz, cc)
        wait_recv(kv.at[yy, zz, cc], kvr.at[2 * n])

    def y_forward(dz):
        kv_arrive(back, dz, c)
        yy, zz, n = kv_index(back, dz, c)
        src = kv.at[yy, zz, c]
        rcopy(src, src, kys.at[dz * 4 + 3], kvr.at[2 * n], at(dy=sign)).start()
        kv_to_sibling(back, dz)

    def y_rest(dz):
        for k in (fwd, 2):
            kv_arrive(k, dz, c)
            kv_to_sibling(k, dz)

    def y_sibling(dz):
        loop(0, 4, lambda k: kv_arrive(k, dz, 1 - c))

    def z_send(dz, half, sem, step):
        yy, zz, n = kv_index(0, dz, c)
        src = kv.at[yy, zz, c, half]
        rcopy(src, src, kzs.at[sem], kvr.at[2 * n + half], at(dz=step)).start()

    def z_arrive(dz, half):
        yy, zz, n = kv_index(0, dz, c)
        wait_recv(kv.at[yy, zz, c, half], kvr.at[2 * n + half])

    own = kv.at[y, zh, c]
    own_half = kv.at[y, zh, c, 0]

    def project(half, w):
        kv[y, zh, c, half] = mm(nrm[...], w[...].reshape(D, HD)).astype(BF)
        z_send(0, half, half, 4 * sign)
        z_send(0, half, 2 + half, -4 * sign)

    sibling_arrive(0)
    project(0, wk)
    second_arrive(3)
    sibling_arrive(3)
    project(1, wv)
    y_send(0)
    ring1_rest(1)
    ring2_send(1)
    ring1_forward(2)
    ring2_forward(1)
    y_forward(0)
    for half in range(2):
        wait_send(own_half, kzs.at[half])
    for half in range(2):
        z_arrive(back, half)
        z_send(back, half, 4 + half, 4 * sign)
    y_send(back)
    y_rest(0)
    ring1_rest(2)
    ring2_send(2)
    ring2_rest(1)
    for half in range(2):
        z_arrive(fwd, half)
    y_send(fwd)
    y_forward(back)
    sibling_arrive(1)

    def make_queries():
        queries = mm(nrm[...], wq[...].reshape(D, ROWS))
        for h in range(HEADS):
            head = queries[:, h * HD : (h + 1) * HD].astype(BF)
            qs[h * TOK : (h + 1) * TOK, :] = head
            qt[:, h * TOK : (h + 1) * TOK] = head.astype(F32).T.astype(BF)

    make_queries()

    mrow[...] = jnp.full((ROWS, 128), -1e30, F32)
    lrow[...] = jnp.zeros((ROWS, 128), F32)
    acc[...] = jnp.zeros((ROWS, HD), F32)

    def forward(k):
        zz = rem4(zh + k)

        def scores():
            for u in range(4):
                keys = kv[u, zz, :, 0].reshape(256, HD)
                sbuf[u] = mm_nt(qs[...], keys)

        scores()

        def rows(start, count):
            rs = pl.ds(start, count)
            peak = mrow[rs, :]
            new = peak
            for u in range(4):
                s = sbuf[u, rs, :]
                new = jnp.maximum(new, jnp.maximum(s[:, :128], s[:, 128:]))
            new = jnp.broadcast_to(jnp.max(new, axis=1, keepdims=True), (count, 128))
            fix = jnp.exp2((peak - new) * LOG2)
            base = new * LOG2
            total = lrow[rs, :] * fix
            for u in range(4):
                s = sbuf[u, rs, :]
                e0 = jnp.exp2(s[:, :128] * LOG2 - base)
                e1 = jnp.exp2(s[:, 128:] * LOG2 - base)
                total = total + (e0 + e1)
                ebuf[k, u, rs, :128] = e0.astype(BF)
                ebuf[k, u, rs, 128:] = e1.astype(BF)
            lrow[rs, :] = total
            mrow[rs, :] = new
            mk[k, rs, :] = new
            acc[rs, :] = acc[rs, :] * fix

        def all_rows(r):
            for part_of in range(4):
                rows(pl.multiple_of(r * 128 + part_of * 32, 32), 32)

        loop(0, 4, all_rows)

        def values():
            total = acc[...]
            for u in range(4):
                total = total + mm(ebuf[k, u], kv[u, zz, :, 1].reshape(256, HD))
            acc[...] = total

        values()

    y_sibling(0)
    forward(0)
    y_forward(fwd)
    ring2_forward(2)
    for half in range(2):
        far_send(half)
    y_rest(back)
    y_rest(fwd)
    y_sibling(1)
    forward(1)
    ring2_rest(2)
    y_sibling(3)
    forward(3)
    for half in range(2):
        far_rest(half)
    sibling_arrive(2)

    def make_d_att():
        d_att = mm_nt(cot_ref[...], wo[...].reshape(ROWS, D)).astype(BF)
        for h in range(HEADS):
            dos[h * TOK : (h + 1) * TOK, :] = d_att[:, h * HD : (h + 1) * HD]

    make_d_att()
    far_sibling()
    forward(2)

    def per_row():
        for h in range(HEADS):
            hs = slice(h * TOK, (h + 1) * TOK)
            mass = jnp.sum(lrow[hs, :], axis=1, keepdims=True)
            inv_l = jnp.broadcast_to(1.0 / mass, (TOK, 128))
            o = acc[hs, :] * inv_l
            att[:, hs] = o.astype(BF)
            top = mrow[hs, :]
            grad = dos[hs, :].astype(F32)
            for k in range(4):
                scaled = (grad * (inv_l * jnp.exp2((mk[k, hs, :] - top) * LOG2))).astype(BF)
                dog[k, hs, :] = scaled
                scaled = scaled.astype(F32)
                delta[k, hs, :] = jnp.broadcast_to(jnp.sum(scaled * o, axis=1, keepdims=True), (TOK, 128))
                dot_[k, :, hs] = scaled.T.astype(BF)

    per_row()

    dq[...] = jnp.zeros((ROWS, HD), F32)

    def unit(d, k):
        unit_compute(d, k)
        n = d * 4 + k
        rcopy(part.at[d, k, 1 - c], sib.at[d, k], rss.at[n], rsr.at[n], sibling).start()

    def unit_compute(d, k):
        yy, zz = rem4(y + k), rem4(zh + d)
        keys, vals = kv[yy, zz, :, 0].reshape(256, HD), kv[yy, zz, :, 1].reshape(256, HD)
        e = ebuf[d, yy]
        dp = mm_nt(dog[d], vals)
        dl = delta[d]
        ef = e.astype(F32)
        ds = jnp.concatenate(
            [ef[:, :128] * (dp[:, :128] - dl), ef[:, 128:] * (dp[:, 128:] - dl)], axis=1
        ).astype(BF)
        dq[...] += mm(ds, keys)
        part[d, k, 0] = (mm(qt[...], ds) * SCALE).astype(BF)
        part[d, k, 1] = mm(dot_[d], e).astype(BF)

    def own_half_of(d, k):
        wait_recv(sib.at[d, k], rsr.at[d * 4 + k])
        return part[d, k, c].astype(F32) + sib[d, k].astype(F32)

    def far_out():
        for half in range(2):
            rows_of = pl.ds(half * 64, 64)
            for k, dst in ((2, yr2), (1, yr1), (3, yr3)):
                if half == 0:
                    mine[2, k] = own_half_of(2, k).astype(BF)
                n = 8 + k + half * 8
                rcopy(
                    mine.at[2, k, rows_of], dst.at[2, rows_of], rys.at[n], ryr.at[n], at(dy=k)
                ).start()

    def far_total():
        total = own_half_of(2, 0)
        for half in range(2):
            rows_of = pl.ds(half * 64, 64)
            part_total = total[half * 64 : (half + 1) * 64, :]
            for k, src in ((1, yr1), (3, yr3), (2, yr2)):
                wait_recv(src.at[2, rows_of], ryr.at[8 + k + half * 8])
                part_total = part_total + src[2, rows_of, :].astype(F32)
            tlow[2, half] = part_total.astype(BF)
            z_out(tlow.at[2, half], zr1.at[half], half, 4 * sign)

    def y_out_direct(d):
        for k, dst in ((2, yr2), (1, yr1), (3, yr3)):
            mine[d, k] = own_half_of(d, k).astype(BF)
            n = d * 4 + k
            rcopy(mine.at[d, k], dst.at[d], rys.at[n], ryr.at[n], at(dy=k)).start()

    def y_total_direct(d):
        total = own_half_of(d, 0)
        for k, src in ((1, yr1), (3, yr3), (2, yr2)):
            wait_recv(src.at[d], ryr.at[d * 4 + k])
            total = total + src[d].astype(F32)
        return total

    def z_out(src, dst, sem, step):
        rcopy(src, dst, rzs.at[sem], rzr.at[sem], at(dz=step)).start()

    def batch(d):
        for k in (2, 1, 3, 0):
            unit(d, k)

    batch(2)
    far_out()
    batch(1)
    y_out_direct(1)
    batch(3)
    y_out_direct(3)
    batch(0)
    far_total()
    y_out_direct(0)
    tsum[1] = y_total_direct(1)
    tsum[3] = y_total_direct(3)
    tlow[back] = tsum[back].astype(BF).reshape(2, 64, 256)
    z_out(tlow.at[back], zr2, 2, -4 * sign)
    for half in range(2):
        wait_recv(zr1.at[half], rzr.at[half])
        tlow[fwd, half] = (tsum[fwd, half * 64 : (half + 1) * 64, :] + zr1[half].astype(F32)).astype(BF)
        z_out(tlow.at[fwd, half], zr3.at[half], 3 + half, 4 * sign)

    def make_dn():
        dqb = jnp.concatenate(
            [(dq[h * TOK : (h + 1) * TOK, :] * SCALE).astype(BF) for h in range(HEADS)], axis=1
        )
        dn[...] = mm_nt(dqb, wq[...].reshape(D, ROWS))

    out_ref[...] = (tok_ref[...].astype(F32) + mm(att[...], wo[...].reshape(ROWS, D))).astype(BF)
    out_copy = pltpu.make_async_copy(out_ref, out_hbm, outs.at[0])
    out_copy.start()
    make_dn()
    total = y_total_direct(0)
    wait_recv(zr2, rzr.at[2])
    for half in range(2):
        wait_recv(zr3.at[half], rzr.at[3 + half])
    total = total + (zr2[...].reshape(128, 256).astype(F32) + zr3[...].reshape(128, 256).astype(F32))
    for t in range(2):
        dtok[t] = total[:, t * TOK : (t + 1) * TOK].T.astype(BF)
    dkv[c] = dtok[c]
    d_copy = rcopy(dtok.at[1 - c], dkv.at[c], ds_, dr_, sibling)
    d_copy.start()

    nt_copy.wait_recv()
    def make_grad():
        grad = mm(nt[0], dtok[0]) + mm(nt[1], dtok[1])
        for zb in range(4):
            for xb in range(4):
                b = zb * 4 + xb
                dx, dz = rem4(xb - x + 4), rem4(zb - zl + 4)
                gr[dx * (1 - c) + dz * c, dz * (1 - c) + dx * c] = grad[b * 96 : (b + 1) * 96, :].astype(BF)

    make_grad()
    for k in (1, 3, 2):
        sh = (1, 2, -1)[k - 1]
        rcopy(gr.at[k], ra.at[k], gas.at[k], gar.at[k], at(dx=k * (1 - c), dz=sh * c)).start()

    d_copy.wait_recv()
    def make_input_grad():
        d_unit = dn[...] + (mm_nt(dkv[0], wk[...].reshape(D, HD)) + mm_nt(dkv[1], wv[...].reshape(D, HD)))
        d_unit = d_unit * gain_ref[...][None, :]
        tok = tok_ref[...].astype(F32)
        inv = lax.rsqrt(jnp.mean(tok * tok, axis=-1, keepdims=True) + EPS)
        unit_rows = tok * inv
        ing_ref[...] = (
            inv * (d_unit - unit_rows * jnp.mean(d_unit * unit_rows, axis=-1, keepdims=True))
        ).astype(BF)

    make_input_grad()
    ing_copy = pltpu.make_async_copy(ing_ref, ing_hbm, outs.at[1])
    ing_copy.start()

    for k in (1, 3, 2):
        wait_recv(ra.at[k], gar.at[k])
    for i in (2, 1, 3, 0):
        gb[i] = (
            (gr[0, i].astype(F32) + ra[1, i].astype(F32)) + (ra[2, i].astype(F32) + ra[3, i].astype(F32))
        ).astype(BF)
        if i:
            sh = (1, 2, -1)[i - 1]
            rcopy(gb.at[i], rb.at[i], gbs.at[i], gbr.at[i], at(dx=i * c, dz=sh * (1 - c))).start()
    for i in (1, 3, 2):
        wait_recv(rb.at[i], gbr.at[i])
    yg[y] = (
        (gb[0].astype(F32) + rb[1].astype(F32)) + (rb[2].astype(F32) + rb[3].astype(F32))
    ).astype(BF)
    for k in (2, 1, 3):
        rcopy(yg.at[y], yg.at[y], ygs.at[k], ygr.at[y], at(dy=k)).start()
    for k in (1, 3, 2):
        wait_recv(yg.at[rem4(y + k)], ygr.at[rem4(y + k)])
    zg[zh] = (
        (yg[0].astype(F32) + yg[1].astype(F32)) + (yg[2].astype(F32) + yg[3].astype(F32))
    ).astype(BF)
    for k, step in ((2, 8), (1, 4), (3, -4)):
        rcopy(zg.at[zh], zg.at[zh], zgs.at[k], zgr.at[zh], at(dz=step)).start()

    for w in range(4):
        weight_sends_done(w)
    nt_copy.wait_send()
    for n in range(2, 6):
        wait_send(own_half, kzs.at[n])

    for dy in range(4):
        for dz in (0, 1, 3):
            wait_send(own, kss.at[dy * 4 + dz])
        wait_send(own_half, kss.at[dy * 4 + 2])
        wait_send(own_half, kss.at[16 + dy])
    for k in (1, 2, 3):
        for d in (0, 1, 3):
            wait_send(own, kys.at[d * 4 + k])
        wait_send(own_half, kys.at[8 + k])
        wait_send(own_half, kys.at[16 + k])

    def part_sends(n):
        d, k = lax.div(n, 4), rem4(n)
        wait_send(part.at[d, k, 1 - c], rss.at[n])

    loop(0, 16, part_sends)
    for k in (1, 2, 3):
        for d in (0, 1, 3):
            wait_send(mine.at[d, k], rys.at[d * 4 + k])
        wait_send(mine.at[2, k, pl.ds(0, 64)], rys.at[8 + k])
        wait_send(mine.at[2, k, pl.ds(64, 64)], rys.at[16 + k])
    for n in (0, 1, 3, 4):
        wait_send(zr1.at[0], rzs.at[n])
    wait_send(zr2, rzs.at[2])
    d_copy.wait_send()
    for k in (1, 2, 3):
        wait_send(gr.at[k], gas.at[k])
        wait_send(gb.at[k], gbs.at[k])
        wait_send(yg.at[y], ygs.at[k])

    for k in (1, 3, 2):
        wait_recv(zg.at[rem4(zh + k)], zgr.at[rem4(zh + k)])
    fin[c] = (
        (zg[0].astype(F32) + zg[1].astype(F32)) + (zg[2].astype(F32) + zg[3].astype(F32))
    ) * (1.0 / 256.0)
    f_copy = rcopy(fin.at[c], fin.at[c], fs, fr, sibling)
    f_copy.start()
    for k in (1, 2, 3):
        wait_send(zg.at[zh], zgs.at[k])
    wait_recv(fin.at[1 - c], fr)
    kvg_ref[:, :HD] = fin[0]
    kvg_ref[:, HD:] = fin[1]
    kvg_copy = pltpu.make_async_copy(kvg_ref, kvg_hbm, outs.at[2])
    kvg_copy.start()
    out_copy.wait()
    ing_copy.wait()
    kvg_copy.wait()
    f_copy.wait_send()


def hand_over(a, b, d, a_out, b_out, d_out, a_buf, b_buf, d_buf, sems):
    moves = ((a, a_buf, a_out), (b, b_buf, b_out), (d, d_buf, d_out))
    reads = [pltpu.make_async_copy(src, buf, sems.at[n]) for n, (src, buf, dst) in enumerate(moves)]
    writes = [pltpu.make_async_copy(buf, dst, sems.at[3 + n]) for n, (src, buf, dst) in enumerate(moves)]
    for copy in reads:
        copy.start()
    for read, write in zip(reads, writes):
        read.wait()
        write.start()
    for copy in writes:
        copy.wait()


def local(tokens, norm_gain, w_query, w_keyval, w_out, cotangent):
    vm = pltpu.VMEM
    dma = pltpu.SemaphoreType.DMA
    scratch = [
        vm((TOK, D), BF), vm((D,), F32), vm((TOK, D), BF), dma((11,)),
        vm((TOK, D), BF), vm((TOK, D), BF), vm((96, 2 * HD), F32), dma((3,)),
        vm((4, 4, 2, 48, HD), BF), vm((4, 4, 2, 48, HD), BF), vm((4, 4, 2, 48, 512), BF), vm((4, 4, 2, 16, D), BF),
        vm((TOK, D), BF), vm((2, D, TOK), BF), vm((4, 4, 2, 2, TOK, HD), BF),
        vm((ROWS, HD), BF), vm((HD, ROWS), BF), vm((4, ROWS, 256), F32), vm((4, 4, ROWS, 256), BF),
        vm((ROWS, HD), F32), vm((ROWS, 128), F32), vm((4, ROWS, 128), F32), vm((ROWS, 128), F32),
        vm((ROWS, HD), BF), vm((4, ROWS, HD), BF), vm((4, HD, ROWS), BF), vm((4, ROWS, 128), F32),
        vm((TOK, ROWS), BF), vm((ROWS, HD), F32),
        vm((4, 4, 2, HD, 256), BF), vm((4, 4, HD, 256), BF), vm((4, 4, HD, 256), BF),
        vm((4, HD, 256), BF), vm((4, HD, 256), BF), vm((4, HD, 256), BF),
        vm((4, HD, 256), F32), vm((4, 2, 64, 256), BF),
        vm((2, 64, 256), BF), vm((2, 64, 256), BF), vm((2, 64, 256), BF),
        vm((2, TOK, HD), BF), vm((2, TOK, HD), BF), vm((TOK, D), F32),
        vm((4, 4, 96, HD), BF), vm((4, 4, 96, HD), BF), vm((4, 96, HD), BF), vm((4, 96, HD), BF),
        vm((4, 96, HD), BF), vm((4, 96, HD), BF), vm((2, 96, HD), F32),
        dma((4, 4)), dma((4, 16)), dma((4, 16)), dma((4, 16)), dma((4, 16)),
        dma((6,)), dma((20,)), dma((20,)), dma((64,)), dma, dma,
        dma((16,)), dma((16,)), dma((20,)), dma((20,)), dma((5,)), dma((5,)), dma, dma,
        dma((4,)), dma((4,)), dma((4,)), dma((4,)), dma((4,)), dma((4,)), dma((4,)), dma((4,)), dma, dma,
    ]
    hbm = pl.BlockSpec(memory_space=pltpu.HBM)
    shapes = (
        jax.ShapeDtypeStruct((TOK, D), BF),
        jax.ShapeDtypeStruct((TOK, D), BF),
        jax.ShapeDtypeStruct((96, 2 * HD), F32),
    )
    results = pl.pallas_call(
        kernel,
        out_shape=shapes,
        in_specs=[hbm] * 6,
        out_specs=(hbm, hbm, hbm),
        scratch_shapes=scratch,
        compiler_params=pltpu.CompilerParams(
            collective_id=0, has_side_effects=True, vmem_limit_bytes=63 * 2**20
        ),
        name="layer",
    )(tokens[0], norm_gain, w_query, w_keyval, w_out, cotangent[0])
    layer_out, input_grad, keyval_grad = pl.pallas_call(
        hand_over,
        out_shape=shapes,
        in_specs=[hbm] * 3,
        out_specs=(hbm, hbm, hbm),
        scratch_shapes=[vm((TOK, D), BF), vm((TOK, D), BF), vm((96, 2 * HD), F32), dma((6,))],
        compiler_params=pltpu.CompilerParams(vmem_limit_bytes=63 * 2**20),
        name="hand_over",
    )(*results)
    return layer_out[None], input_grad[None], keyval_grad


def solution(mesh):
    placed = (
        P("batch", "seq", None),
        P(),
        P("batch", None),
        P("batch", None),
        P("batch", None),
        P("batch", "seq", None),
    )
    return jax.shard_map(
        local,
        mesh=mesh,
        in_specs=placed,
        out_specs=(P("batch", "seq", None), P("batch", "seq", None), P("batch", None)),
        check_vma=False,
    )
```

```python
import math

import jax
import jax.numpy as jnp
from jax import lax
from jax.experimental import pallas as pl
from jax.experimental.pallas import tpu as pltpu
from jax.sharding import PartitionSpec as P

MESH = pl.DeviceIdType.MESH
BF, F32 = jnp.bfloat16, jnp.float32
EPS = 1e-06
HD, HEADS, TOK, D = 128, 4, 128, 1536
ROWS = HEADS * TOK
SCALE = 1.0 / math.sqrt(HD)
LOG2 = SCALE * math.log2(math.e)
NT_DIMS = (((1,), (1,)), ((), ()))


def mm(a, b):
    return jnp.dot(a, b, preferred_element_type=F32)


def mm_nt(a, b):
    return lax.dot_general(a, b, NT_DIMS, preferred_element_type=F32)


def rem4(v):
    return lax.rem(v, 4)


def kernel(
    tok_hbm, gain_hbm, wq_hbm, wkv_hbm, wo_hbm, cot_hbm,
    out_hbm, ing_hbm, kvg_hbm,
    tok_ref, gain_ref, cot_ref, ins, out_ref, ing_ref, kvg_ref, outs,
    wk, wv, wq, wo, nrm, nt, kv, qs, qt, sbuf, ebuf, acc, mrow, mk, lrow,
    dos, dog, dot_, delta, att, dq, part, sib, mine, yr1, yr2, yr3, tsum, tlow, zr1, zr2, zr3,
    dtok, dkv, dn, gr, ra, gb, rb, yg, zg, fin,
    w1s, w2s, wss, wr, wsr, kzs, kys, kss, kvr, nts, ntr,
    rss, rsr, rys, ryr, rzs, rzr, ds_, dr_, gas, gar, gbs, gbr, ygs, ygr, zgs, zgr, fs, fr,
):
    bi = lax.axis_index("batch")
    si = lax.axis_index("seq")
    zl, x = lax.div(bi, 4), rem4(bi)
    y, zh, c = lax.div(si, 8), rem4(lax.div(si, 2)), lax.rem(si, 2)

    def at(dx=0, dy=0, dz=0, dc=0):
        z = lax.rem(zh * 4 + zl + dz + 16, 16)
        return (
            rem4(z) * 4 + rem4(x + dx + 4),
            rem4(y + dy + 4) * 8 + lax.div(z, 4) * 2 + lax.rem(c + dc, 2),
        )

    sibling = at(dc=1)
    fwd, back = 1 + 2 * c, 3 - 2 * c
    sign = 1 - 2 * c

    def rcopy(src, dst, ssem, rsem, device):
        return pltpu.make_async_remote_copy(
            src_ref=src, dst_ref=dst, send_sem=ssem, recv_sem=rsem, device_id=device, device_id_type=MESH
        )

    def wait_recv(ref, rsem):
        rcopy(ref, ref, rsem, rsem, sibling).wait_recv()

    def wait_send(ref, ssem):
        rcopy(ref, ref, ssem, ssem, sibling).wait_send()

    def loop(lo, hi, body):
        def step(i, carry):
            body(i)
            return carry

        lax.fori_loop(lo, hi, step, 0)

    barrier = pltpu.get_barrier_semaphore()
    partners = [at(dc=1)]
    partners += [at(dx=k) for k in (1, 2, 3)]
    partners += [at(dy=k) for k in (1, 2, 3)]
    partners += [at(dz=k) for k in (1, -1, 2, -2, 4, -4)]
    for p in partners:
        pl.semaphore_signal(barrier, inc=1, device_id=p, device_id_type=MESH)

    loads = [
        pltpu.make_async_copy(tok_hbm, tok_ref, ins.at[0]),
        pltpu.make_async_copy(gain_hbm, gain_ref, ins.at[1]),
    ]
    own_parts = ((wkv_hbm, wk, 48, 0, HD), (wkv_hbm, wv, 48, HD, HD), (wq_hbm, wq, 48, 0, ROWS), (wo_hbm, wo, 16, 0, D))
    for n, (w_hbm, w, h, col, width) in enumerate(own_parts):
        for half in range(2):
            src = w_hbm.at[pl.ds(half * h, h), pl.ds(col, width)]
            loads.append(pltpu.make_async_copy(src, w.at[zl, x, half], ins.at[2 + 2 * n + half]))
    loads.append(pltpu.make_async_copy(cot_hbm, cot_ref, ins.at[10]))
    for load in loads:
        load.start()

    def norm():
        tok = tok_ref[...].astype(F32)
        inv = lax.rsqrt(jnp.mean(tok * tok, axis=-1, keepdims=True) + EPS)
        normed = tok * inv * gain_ref[...][None, :]
        nrm[...] = normed.astype(BF)

    def norm_t():
        for i in range(D // 128):
            nt[c, i * 128 : (i + 1) * 128, :] = nrm[:, i * 128 : (i + 1) * 128].astype(F32).T.astype(BF)

    for load in loads[2:10]:
        load.wait()
    pl.semaphore_wait(barrier, len(partners))

    one = c * 0 + 1
    zero = c * 0
    weights = ((wk, c, 1 - c), (wq, zero, one), (wo, zero, one), (wv, c, 1 - c))

    def block(w, i, j):
        ref, ax, az = weights[w]
        zz, xx = rem4(zl + i * az + j * ax), rem4(x + i * ax + j * az)
        return ref.at[zz, xx, c], zz * 4 + xx

    def other_half(w, i, j):
        ref, ax, az = weights[w]
        zz, xx = rem4(zl + i * az + j * ax), rem4(x + i * ax + j * az)
        return ref.at[zz, xx, 1 - c], zz * 4 + xx

    def zshift(k):
        return rem4(k + 1) - 1

    def first_send(w):
        ref, ax, az = weights[w]

        def body(k):
            src, idx = block(w, 0, 0)
            rcopy(src, src, w1s.at[w, k], wr.at[w, idx], at(dx=k * ax, dz=zshift(k) * az)).start()

        loop(1, 4, body)

    def to_sibling(w, i, j):
        src, idx = block(w, i, j)
        rcopy(src, src, wss.at[w, idx], wsr.at[w, idx], sibling).start()

    def first_arrive(w):
        def body(i):
            src, idx = block(w, i, 0)
            wait_recv(src, wr.at[w, idx])

        loop(1, 4, body)

    def second_send(w):
        ref, ax, az = weights[w]

        def body(i):
            src, idx = block(w, i, 0)
            for k in (1, 3, 2):
                rcopy(src, src, w2s.at[w, i * 4 + k], wr.at[w, idx], at(dx=k * az, dz=zshift(k) * ax)).start()

        loop(0, 4, body)
        loop(1, 4, lambda i: to_sibling(w, i, 0))

    def second_arrive(w):
        for j in (1, 3, 2):

            def body(i, j=j):
                src, idx = block(w, i, j)
                wait_recv(src, wr.at[w, idx])
                to_sibling(w, i, j)

            loop(0, 4, body)

    def sibling_arrive(w):
        def body(n):
            src, idx = other_half(w, rem4(n), lax.div(n, 4))
            wait_recv(src, wsr.at[w, idx])

        loop(1, 16, body)

    def weight_sends_done(w):
        def body1(k):
            src, idx = block(w, 0, 0)
            wait_send(src, w1s.at[w, k])

        loop(1, 4, body1)

        def body2(i):
            src, idx = block(w, i, 0)
            for k in (1, 2, 3):
                wait_send(src, w2s.at[w, i * 4 + k])

        loop(0, 4, body2)

        def body3(n):
            src, idx = block(w, rem4(n), lax.div(n, 4))
            wait_send(src, wss.at[w, idx])

        loop(1, 16, body3)

    def ring1_send(w):
        src, idx = block(w, 0, 0)
        for n, step in ((1, 1), (2, -1)):
            rcopy(src, src, w1s.at[w, n], wr.at[w, idx], at(dz=step)).start()

    def ring1_forward(w):
        src, idx = block(w, back, 0)
        wait_recv(src, wr.at[w, idx])
        rcopy(src, src, w1s.at[w, 3], wr.at[w, idx], at(dz=sign)).start()

    def ring1_rest(w):
        for i in (fwd, 2):
            src, idx = block(w, i, 0)
            wait_recv(src, wr.at[w, idx])

    def ring2_send(w):
        def body(i):
            src, idx = block(w, i, 0)
            for n, step in ((1, 1), (2, -1)):
                rcopy(src, src, w2s.at[w, i * 4 + n], wr.at[w, idx], at(dx=step)).start()

        loop(0, 4, body)
        loop(1, 4, lambda i: to_sibling(w, i, 0))

    def ring2_forward(w):
        def body(i):
            src, idx = block(w, i, back)
            wait_recv(src, wr.at[w, idx])
            rcopy(src, src, w2s.at[w, i * 4 + 3], wr.at[w, idx], at(dx=sign)).start()
            to_sibling(w, i, back)

        loop(0, 4, body)

    def ring2_rest(w):
        for j in (fwd, 2):

            def body(i, j=j):
                src, idx = block(w, i, j)
                wait_recv(src, wr.at[w, idx])
                to_sibling(w, i, j)

            loop(0, 4, body)

    first_send(0)
    first_send(3)
    ring1_send(1)
    for load in (loads[0], loads[1], loads[10]):
        load.wait()
    norm()
    norm_t()
    first_arrive(0)
    second_send(0)
    first_arrive(3)
    second_send(3)
    nt_copy = rcopy(nt.at[c], nt.at[c], nts, ntr, sibling)
    nt_copy.start()
    ring1_forward(1)
    ring1_send(2)
    second_arrive(0)

    def kv_index(dy, dz, cc):
        yy, zz = rem4(y + dy), rem4(zh + dz)
        return yy, zz, (yy * 4 + zz) * 2 + cc

    def kv_to_sibling(dy, dz):
        yy, zz, n = kv_index(dy, dz, c)
        src = kv.at[yy, zz, c]
        rcopy(src, src, kss.at[dy * 4 + dz], kvr.at[2 * n], sibling).start()

    def half_to_sibling(dy, half):
        yy, zz, n = kv_index(dy, 2, c)
        src = kv.at[yy, zz, c, half]
        rcopy(src, src, kss.at[dy * 4 + 2 + half * (14 - 3 * dy)], kvr.at[2 * n + half], sibling).start()

    def half_arrive(dy, half, cc):
        yy, zz, n = kv_index(dy, 2, cc)
        wait_recv(kv.at[yy, zz, cc, half], kvr.at[2 * n + half])

    def far_send(half):
        yy, zz, n = kv_index(0, 2, c)
        src = kv.at[yy, zz, c, half]
        half_arrive(0, half, c)
        for k, step in ((3, 2), (1, 1), (2, -1)):
            rcopy(src, src, kys.at[8 + k + half * 8], kvr.at[2 * n + half], at(dy=step)).start()
        half_to_sibling(0, half)

    def far_rest(half):
        for dy in (1, 3, 2):
            half_arrive(dy, half, c)
            half_to_sibling(dy, half)

    def far_sibling():
        for half in range(2):
            for dy in range(4):
                half_arrive(dy, half, 1 - c)

    def y_send(dz, direct=False):
        yy, zz, n = kv_index(0, dz, c)
        src = kv.at[yy, zz, c]
        for k, step in ((3, 2), (1, 1), (2, -1)) if direct else ((1, 1), (2, -1)):
            rcopy(src, src, kys.at[dz * 4 + k], kvr.at[2 * n], at(dy=step)).start()
        kv_to_sibling(0, dz)

    def kv_arrive(dy, dz, cc):
        yy, zz, n = kv_index(dy, dz, cc)
        wait_recv(kv.at[yy, zz, cc], kvr.at[2 * n])

    def y_forward(dz):
        kv_arrive(back, dz, c)
        yy, zz, n = kv_index(back, dz, c)
        src = kv.at[yy, zz, c]
        rcopy(src, src, kys.at[dz * 4 + 3], kvr.at[2 * n], at(dy=sign)).start()
        kv_to_sibling(back, dz)

    def y_rest(dz, direct=False):
        for k in (back, fwd, 2) if direct else (fwd, 2):
            kv_arrive(k, dz, c)
            kv_to_sibling(k, dz)

    def y_sibling(dz):
        loop(0, 4, lambda k: kv_arrive(k, dz, 1 - c))

    def z_send(dz, half, sem, step):
        yy, zz, n = kv_index(0, dz, c)
        src = kv.at[yy, zz, c, half]
        rcopy(src, src, kzs.at[sem], kvr.at[2 * n + half], at(dz=step)).start()

    def z_arrive(dz, half):
        yy, zz, n = kv_index(0, dz, c)
        wait_recv(kv.at[yy, zz, c, half], kvr.at[2 * n + half])

    own = kv.at[y, zh, c]
    own_half = kv.at[y, zh, c, 0]

    def project(half, w):
        kv[y, zh, c, half] = mm(nrm[...], w[...].reshape(D, HD)).astype(BF)
        z_send(0, half, half, 4 * sign)
        z_send(0, half, 2 + half, -4 * sign)

    sibling_arrive(0)
    project(0, wk)
    second_arrive(3)
    sibling_arrive(3)
    project(1, wv)
    y_send(0, direct=True)
    ring1_rest(1)
    ring2_send(1)
    ring1_forward(2)
    ring2_forward(1)
    for half in range(2):
        z_arrive(back, half)
        z_send(back, half, 4 + half, 4 * sign)
    y_send(back, direct=True)
    y_rest(0, direct=True)
    ring1_rest(2)
    ring2_send(2)
    ring2_rest(1)
    for half in range(2):
        z_arrive(fwd, half)
    y_send(fwd, direct=True)
    sibling_arrive(1)

    def make_queries():
        queries = mm(nrm[...], wq[...].reshape(D, ROWS))
        for h in range(HEADS):
            head = queries[:, h * HD : (h + 1) * HD].astype(BF)
            qs[h * TOK : (h + 1) * TOK, :] = head
            qt[:, h * TOK : (h + 1) * TOK] = head.astype(F32).T.astype(BF)

    make_queries()

    mrow[...] = jnp.full((ROWS, 128), -1e30, F32)
    lrow[...] = jnp.zeros((ROWS, 128), F32)
    acc[...] = jnp.zeros((ROWS, HD), F32)

    def forward(k):
        zz = rem4(zh + k)

        def scores():
            for u in range(4):
                keys = kv[u, zz, :, 0].reshape(256, HD)
                sbuf[u] = mm_nt(qs[...], keys)

        scores()

        def rows(start, count):
            rs = pl.ds(start, count)
            peak = mrow[rs, :]
            new = peak
            for u in range(4):
                s = sbuf[u, rs, :]
                new = jnp.maximum(new, jnp.maximum(s[:, :128], s[:, 128:]))
            new = jnp.broadcast_to(jnp.max(new, axis=1, keepdims=True), (count, 128))
            fix = jnp.exp2((peak - new) * LOG2)
            base = new * LOG2
            total = lrow[rs, :] * fix
            for u in range(4):
                s = sbuf[u, rs, :]
                e0 = jnp.exp2(s[:, :128] * LOG2 - base)
                e1 = jnp.exp2(s[:, 128:] * LOG2 - base)
                total = total + (e0 + e1)
                ebuf[k, u, rs, :128] = e0.astype(BF)
                ebuf[k, u, rs, 128:] = e1.astype(BF)
            lrow[rs, :] = total
            mrow[rs, :] = new
            mk[k, rs, :] = new
            acc[rs, :] = acc[rs, :] * fix

        def all_rows(r):
            for part_of in range(4):
                rows(pl.multiple_of(r * 128 + part_of * 32, 32), 32)

        loop(0, 4, all_rows)

        def values():
            total = acc[...]
            for u in range(4):
                total = total + mm(ebuf[k, u], kv[u, zz, :, 1].reshape(256, HD))
            acc[...] = total

        values()

    y_sibling(0)
    forward(0)
    ring2_forward(2)
    for half in range(2):
        far_send(half)
    y_rest(back, direct=True)
    y_rest(fwd, direct=True)
    y_sibling(1)
    forward(1)
    ring2_rest(2)
    y_sibling(3)
    forward(3)
    for half in range(2):
        far_rest(half)
    sibling_arrive(2)

    def make_d_att():
        d_att = mm_nt(cot_ref[...], wo[...].reshape(ROWS, D)).astype(BF)
        for h in range(HEADS):
            dos[h * TOK : (h + 1) * TOK, :] = d_att[:, h * HD : (h + 1) * HD]

    make_d_att()
    far_sibling()
    forward(2)

    def per_row():
        for h in range(HEADS):
            hs = slice(h * TOK, (h + 1) * TOK)
            mass = jnp.sum(lrow[hs, :], axis=1, keepdims=True)
            inv_l = jnp.broadcast_to(1.0 / mass, (TOK, 128))
            o = acc[hs, :] * inv_l
            att[:, hs] = o.astype(BF)
            top = mrow[hs, :]
            grad = dos[hs, :].astype(F32)
            for k in range(4):
                scaled = (grad * (inv_l * jnp.exp2((mk[k, hs, :] - top) * LOG2))).astype(BF)
                dog[k, hs, :] = scaled
                scaled = scaled.astype(F32)
                delta[k, hs, :] = jnp.broadcast_to(jnp.sum(scaled * o, axis=1, keepdims=True), (TOK, 128))
                dot_[k, :, hs] = scaled.T.astype(BF)

    per_row()

    dq[...] = jnp.zeros((ROWS, HD), F32)

    def unit(d, k):
        unit_compute(d, k)
        n = d * 4 + k
        rcopy(part.at[d, k, 1 - c], sib.at[d, k], rss.at[n], rsr.at[n], sibling).start()

    def unit_compute(d, k):
        yy, zz = rem4(y + k), rem4(zh + d)
        keys, vals = kv[yy, zz, :, 0].reshape(256, HD), kv[yy, zz, :, 1].reshape(256, HD)
        e = ebuf[d, yy]
        dp = mm_nt(dog[d], vals)
        dl = delta[d]
        ef = e.astype(F32)
        ds = jnp.concatenate(
            [ef[:, :128] * (dp[:, :128] - dl), ef[:, 128:] * (dp[:, 128:] - dl)], axis=1
        ).astype(BF)
        dq[...] += mm(ds, keys)
        part[d, k, 0] = (mm(qt[...], ds) * SCALE).astype(BF)
        part[d, k, 1] = mm(dot_[d], e).astype(BF)

    def own_half_of(d, k):
        wait_recv(sib.at[d, k], rsr.at[d * 4 + k])
        return part[d, k, c].astype(F32) + sib[d, k].astype(F32)

    def far_out():
        for half in range(2):
            rows_of = pl.ds(half * 64, 64)
            for k, dst in ((2, yr2), (1, yr1), (3, yr3)):
                if half == 0:
                    mine[2, k] = own_half_of(2, k).astype(BF)
                n = 8 + k + half * 8
                rcopy(
                    mine.at[2, k, rows_of], dst.at[2, rows_of], rys.at[n], ryr.at[n], at(dy=k)
                ).start()

    def far_total():
        total = own_half_of(2, 0)
        for half in range(2):
            rows_of = pl.ds(half * 64, 64)
            part_total = total[half * 64 : (half + 1) * 64, :]
            for k, src in ((1, yr1), (3, yr3), (2, yr2)):
                wait_recv(src.at[2, rows_of], ryr.at[8 + k + half * 8])
                part_total = part_total + src[2, rows_of, :].astype(F32)
            tlow[2, half] = part_total.astype(BF)
            z_out(tlow.at[2, half], zr1.at[half], half, 4 * sign)

    def y_out_direct(d):
        for k, dst in ((2, yr2), (1, yr1), (3, yr3)):
            mine[d, k] = own_half_of(d, k).astype(BF)
            n = d * 4 + k
            rcopy(mine.at[d, k], dst.at[d], rys.at[n], ryr.at[n], at(dy=k)).start()

    def y_total_direct(d):
        total = own_half_of(d, 0)
        for k, src in ((1, yr1), (3, yr3), (2, yr2)):
            wait_recv(src.at[d], ryr.at[d * 4 + k])
            total = total + src[d].astype(F32)
        return total

    def z_out(src, dst, sem, step):
        rcopy(src, dst, rzs.at[sem], rzr.at[sem], at(dz=step)).start()

    def batch(d):
        for k in (2, 1, 3, 0):
            unit(d, k)

    batch(2)
    far_out()
    batch(1)
    y_out_direct(1)
    batch(3)
    y_out_direct(3)
    batch(0)
    far_total()
    y_out_direct(0)
    tsum[1] = y_total_direct(1)
    tsum[3] = y_total_direct(3)
    tlow[back] = tsum[back].astype(BF).reshape(2, 64, 256)
    z_out(tlow.at[back], zr2, 2, -4 * sign)
    for half in range(2):
        wait_recv(zr1.at[half], rzr.at[half])
        tlow[fwd, half] = (tsum[fwd, half * 64 : (half + 1) * 64, :] + zr1[half].astype(F32)).astype(BF)
        z_out(tlow.at[fwd, half], zr3.at[half], 3 + half, 4 * sign)

    def make_dn():
        dqb = jnp.concatenate(
            [(dq[h * TOK : (h + 1) * TOK, :] * SCALE).astype(BF) for h in range(HEADS)], axis=1
        )
        dn[...] = mm_nt(dqb, wq[...].reshape(D, ROWS))

    out_ref[...] = (tok_ref[...].astype(F32) + mm(att[...], wo[...].reshape(ROWS, D))).astype(BF)
    out_copy = pltpu.make_async_copy(out_ref, out_hbm, outs.at[0])
    out_copy.start()
    make_dn()
    total = y_total_direct(0)
    wait_recv(zr2, rzr.at[2])
    for half in range(2):
        wait_recv(zr3.at[half], rzr.at[3 + half])
    total = total + (zr2[...].reshape(128, 256).astype(F32) + zr3[...].reshape(128, 256).astype(F32))
    for t in range(2):
        dtok[t] = total[:, t * TOK : (t + 1) * TOK].T.astype(BF)
    dkv[c] = dtok[c]
    d_copy = rcopy(dtok.at[1 - c], dkv.at[c], ds_, dr_, sibling)
    d_copy.start()

    nt_copy.wait_recv()
    def make_grad():
        grad = mm(nt[0], dtok[0]) + mm(nt[1], dtok[1])
        for zb in range(4):
            for xb in range(4):
                b = zb * 4 + xb
                dx, dz = rem4(xb - x + 4), rem4(zb - zl + 4)
                gr[dx * (1 - c) + dz * c, dz * (1 - c) + dx * c] = grad[b * 96 : (b + 1) * 96, :].astype(BF)

    make_grad()
    for i in (2, 1, 3, 0):
        for k in (2, 1, 3):
            sh = (1, 2, -1)[k - 1]
            n = k * 4 + i
            rcopy(gr.at[k, i], ra.at[k, i], gas.at[n], gar.at[n], at(dx=k * (1 - c), dz=sh * c)).start()

    d_copy.wait_recv()
    def make_input_grad():
        d_unit = dn[...] + (mm_nt(dkv[0], wk[...].reshape(D, HD)) + mm_nt(dkv[1], wv[...].reshape(D, HD)))
        d_unit = d_unit * gain_ref[...][None, :]
        tok = tok_ref[...].astype(F32)
        inv = lax.rsqrt(jnp.mean(tok * tok, axis=-1, keepdims=True) + EPS)
        unit_rows = tok * inv
        ing_ref[...] = (
            inv * (d_unit - unit_rows * jnp.mean(d_unit * unit_rows, axis=-1, keepdims=True))
        ).astype(BF)

    make_input_grad()
    ing_copy = pltpu.make_async_copy(ing_ref, ing_hbm, outs.at[1])
    ing_copy.start()

    for i in (2, 1, 3, 0):
        for k in (1, 3, 2):
            wait_recv(ra.at[k, i], gar.at[k * 4 + i])
        gb[i] = (
            (gr[0, i].astype(F32) + ra[1, i].astype(F32)) + (ra[2, i].astype(F32) + ra[3, i].astype(F32))
        ).astype(BF)
        if i:
            sh = (1, 2, -1)[i - 1]
            rcopy(gb.at[i], rb.at[i], gbs.at[i], gbr.at[i], at(dx=i * c, dz=sh * (1 - c))).start()
    for i in (1, 3, 2):
        wait_recv(rb.at[i], gbr.at[i])
    yg[y] = (
        (gb[0].astype(F32) + rb[1].astype(F32)) + (rb[2].astype(F32) + rb[3].astype(F32))
    ).astype(BF)
    for k in (2, 1, 3):
        rcopy(yg.at[y], yg.at[y], ygs.at[k], ygr.at[y], at(dy=k)).start()
    for k in (1, 3, 2):
        wait_recv(yg.at[rem4(y + k)], ygr.at[rem4(y + k)])
    zg[zh] = (
        (yg[0].astype(F32) + yg[1].astype(F32)) + (yg[2].astype(F32) + yg[3].astype(F32))
    ).astype(BF)
    for k, step in ((2, 8), (1, 4), (3, -4)):
        rcopy(zg.at[zh], zg.at[zh], zgs.at[k], zgr.at[zh], at(dz=step)).start()

    for w in range(4):
        weight_sends_done(w)
    nt_copy.wait_send()
    for n in range(6):
        wait_send(own_half, kzs.at[n])

    for dy in range(4):
        for dz in (0, 1, 3):
            wait_send(own, kss.at[dy * 4 + dz])
        wait_send(own_half, kss.at[dy * 4 + 2])
        wait_send(own_half, kss.at[16 + dy])
    for k in (1, 2, 3):
        for d in (0, 1, 3):
            wait_send(own, kys.at[d * 4 + k])
        wait_send(own_half, kys.at[8 + k])
        wait_send(own_half, kys.at[16 + k])

    def part_sends(n):
        d, k = lax.div(n, 4), rem4(n)
        wait_send(part.at[d, k, 1 - c], rss.at[n])

    loop(0, 16, part_sends)
    for k in (1, 2, 3):
        for d in (0, 1, 3):
            wait_send(mine.at[d, k], rys.at[d * 4 + k])
        wait_send(mine.at[2, k, pl.ds(0, 64)], rys.at[8 + k])
        wait_send(mine.at[2, k, pl.ds(64, 64)], rys.at[16 + k])
    for n in (0, 1, 3, 4):
        wait_send(zr1.at[0], rzs.at[n])
    wait_send(zr2, rzs.at[2])
    d_copy.wait_send()
    for k in (1, 2, 3):
        for i in range(4):
            wait_send(gr.at[k, i], gas.at[k * 4 + i])
        wait_send(gb.at[k], gbs.at[k])
        wait_send(yg.at[y], ygs.at[k])

    for k in (1, 3, 2):
        wait_recv(zg.at[rem4(zh + k)], zgr.at[rem4(zh + k)])
    fin[c] = (
        (zg[0].astype(F32) + zg[1].astype(F32)) + (zg[2].astype(F32) + zg[3].astype(F32))
    ) * (1.0 / 256.0)
    f_copy = rcopy(fin.at[c], fin.at[c], fs, fr, sibling)
    f_copy.start()
    for k in (1, 2, 3):
        wait_send(zg.at[zh], zgs.at[k])
    wait_recv(fin.at[1 - c], fr)
    kvg_ref[:, :HD] = fin[0]
    kvg_ref[:, HD:] = fin[1]
    kvg_copy = pltpu.make_async_copy(kvg_ref, kvg_hbm, outs.at[2])
    kvg_copy.start()
    out_copy.wait()
    ing_copy.wait()
    kvg_copy.wait()
    f_copy.wait_send()


def hand_over(a, b, d, a_out, b_out, d_out, a_buf, b_buf, d_buf, sems):
    moves = ((a, a_buf, a_out), (b, b_buf, b_out), (d, d_buf, d_out))
    reads = [pltpu.make_async_copy(src, buf, sems.at[n]) for n, (src, buf, dst) in enumerate(moves)]
    writes = [pltpu.make_async_copy(buf, dst, sems.at[3 + n]) for n, (src, buf, dst) in enumerate(moves)]
    for copy in reads:
        copy.start()
    for read, write in zip(reads, writes):
        read.wait()
        write.start()
    for copy in writes:
        copy.wait()


def local(tokens, norm_gain, w_query, w_keyval, w_out, cotangent):
    vm = pltpu.VMEM
    dma = pltpu.SemaphoreType.DMA
    scratch = [
        vm((TOK, D), BF), vm((D,), F32), vm((TOK, D), BF), dma((11,)),
        vm((TOK, D), BF), vm((TOK, D), BF), vm((96, 2 * HD), F32), dma((3,)),
        vm((4, 4, 2, 48, HD), BF), vm((4, 4, 2, 48, HD), BF), vm((4, 4, 2, 48, 512), BF), vm((4, 4, 2, 16, D), BF),
        vm((TOK, D), BF), vm((2, D, TOK), BF), vm((4, 4, 2, 2, TOK, HD), BF),
        vm((ROWS, HD), BF), vm((HD, ROWS), BF), vm((4, ROWS, 256), F32), vm((4, 4, ROWS, 256), BF),
        vm((ROWS, HD), F32), vm((ROWS, 128), F32), vm((4, ROWS, 128), F32), vm((ROWS, 128), F32),
        vm((ROWS, HD), BF), vm((4, ROWS, HD), BF), vm((4, HD, ROWS), BF), vm((4, ROWS, 128), F32),
        vm((TOK, ROWS), BF), vm((ROWS, HD), F32),
        vm((4, 4, 2, HD, 256), BF), vm((4, 4, HD, 256), BF), vm((4, 4, HD, 256), BF),
        vm((4, HD, 256), BF), vm((4, HD, 256), BF), vm((4, HD, 256), BF),
        vm((4, HD, 256), F32), vm((4, 2, 64, 256), BF),
        vm((2, 64, 256), BF), vm((2, 64, 256), BF), vm((2, 64, 256), BF),
        vm((2, TOK, HD), BF), vm((2, TOK, HD), BF), vm((TOK, D), F32),
        vm((4, 4, 96, HD), BF), vm((4, 4, 96, HD), BF), vm((4, 96, HD), BF), vm((4, 96, HD), BF),
        vm((4, 96, HD), BF), vm((4, 96, HD), BF), vm((2, 96, HD), F32),
        dma((4, 4)), dma((4, 16)), dma((4, 16)), dma((4, 16)), dma((4, 16)),
        dma((6,)), dma((20,)), dma((20,)), dma((64,)), dma, dma,
        dma((16,)), dma((16,)), dma((20,)), dma((20,)), dma((5,)), dma((5,)), dma, dma,
        dma((16,)), dma((16,)), dma((4,)), dma((4,)), dma((4,)), dma((4,)), dma((4,)), dma((4,)), dma, dma,
    ]
    hbm = pl.BlockSpec(memory_space=pltpu.HBM)
    shapes = (
        jax.ShapeDtypeStruct((TOK, D), BF),
        jax.ShapeDtypeStruct((TOK, D), BF),
        jax.ShapeDtypeStruct((96, 2 * HD), F32),
    )
    results = pl.pallas_call(
        kernel,
        out_shape=shapes,
        in_specs=[hbm] * 6,
        out_specs=(hbm, hbm, hbm),
        scratch_shapes=scratch,
        compiler_params=pltpu.CompilerParams(
            collective_id=0, has_side_effects=True, vmem_limit_bytes=63 * 2**20
        ),
        name="layer",
    )(tokens[0], norm_gain, w_query, w_keyval, w_out, cotangent[0])
    layer_out, input_grad, keyval_grad = pl.pallas_call(
        hand_over,
        out_shape=shapes,
        in_specs=[hbm] * 3,
        out_specs=(hbm, hbm, hbm),
        scratch_shapes=[vm((TOK, D), BF), vm((TOK, D), BF), vm((96, 2 * HD), F32), dma((6,))],
        compiler_params=pltpu.CompilerParams(vmem_limit_bytes=63 * 2**20),
        name="hand_over",
    )(*results)
    return layer_out[None], input_grad[None], keyval_grad


def solution(mesh):
    placed = (
        P("batch", "seq", None),
        P(),
        P("batch", None),
        P("batch", None),
        P("batch", None),
        P("batch", "seq", None),
    )
    return jax.shard_map(
        local,
        mesh=mesh,
        in_specs=placed,
        out_specs=(P("batch", "seq", None), P("batch", "seq", None), P("batch", None)),
        check_vma=False,
    )
```
